768 devices in a mesh: grp: 32 (over x, y), shard: 24 (over z, core).
Axes of the slice: x: 4, y: 8, z: 12, core: 2. Of those that a mesh axis runs over, the one named last changes fastest.
Arguments:
- table: float32 [393216, 128], P(('grp', 'shard')), may hold values from -6 to 6
- hot_offsets: int32 [12288], P(('grp', 'shard')), may hold values from 0 to 511, as said below
- cold_dest: int32 [6144], P(('grp', 'shard')), may hold values from 0 to 23, as said below
- bag_ids: int32 [24576, 16], P(('grp', 'shard')), may hold values from 0 to 24575, as said below
- bag_len: int32 [24576], P(('grp', 'shard')), may hold values from 1 to 16, as said below
Outputs:
- new_table: float32 [393216, 128], P(('grp', 'shard'))
- pooled: float32 [24576, 128], P(('grp', 'shard'))
The draws below stay inside these ranges and needn't reach their ends.
Inputs may be any that keep to these rules, and one draw needn't show every extreme that they name: `hot_offsets`: the 16 entries of one device are distinct offsets into that device's own 512 rows. `cold_dest`: entries of device (g, s) are that device's 8 blocks in order. Every device sends exactly 2 blocks to each of 4 devices of its group and none to the others, and every device receives exactly 8 blocks. `bag_ids`: ids below 12288 name hot rows; the others are 12288 plus a row of the sample's own group. Call hot id h's shard index (h // 16) % 24 and cold id i's shard index (i - 12288) // 512. Of the 512 slots of one device, live or not, at most 27 have ids of any one shard index, and in every device exactly 27 have ids of one shard index. `bag_len`: the first sample of each device has 16 live slots.
All inputs are finite; a program needn't handle non-finite values.
Results may differ from the reference program's by a relative error of at most 0.0003.
Values sent between devices are 32-bit elements; how exact they have to be, the bound alone decides.
A program may use at most 32 MiB of HBM per device.

```python
import jax
import jax.numpy as jnp
from jax import lax

DIM = 128
TR = 512
BLK = 64
HOT_DEV = 16
SAMP_DEV = 32
BAG = 16
NB = 8
CAP = 2
FCAP = 27
HOT = 12288
ROWS_G = 12288
ROWS = 393216
SAMP_G = 768
SAMP = 24576
N_GRP = 32
N_SHARD = 24


def draw_hot_offsets(key, part):
    key = jax.random.fold_in(key, 11)
    keys = jax.random.split(key, N_GRP * N_SHARD)
    picked = jax.vmap(lambda k: jax.random.permutation(k, TR)[:HOT_DEV])(keys)
    return picked.reshape(-1).astype(jnp.int32)


def draw_cold_dest(key, part):
    key = jax.random.fold_in(key, 23)
    key_sets, key_orders = jax.random.split(key)
    count = NB // CAP
    offsets = jax.vmap(lambda k: jax.random.permutation(k, N_SHARD)[:count])(jax.random.split(key_sets, N_GRP))
    orders = jax.vmap(lambda k: jax.random.permutation(k, NB))(jax.random.split(key_orders, N_GRP * N_SHARD))
    orders = orders.reshape(N_GRP, N_SHARD, NB) // CAP
    spread = jnp.broadcast_to(offsets[:, None, :], (N_GRP, N_SHARD, count))
    chosen = jnp.take_along_axis(spread, orders, axis=2)
    shard_index = jnp.arange(N_SHARD, dtype=jnp.int32)[None, :, None]
    return ((shard_index + chosen) % N_SHARD).reshape(-1).astype(jnp.int32)


def draw_bag_ids(key, part):
    key = jax.random.fold_in(key, 37)
    key_pick, key_left, key_right, key_cold, key_heavy, key_perm = jax.random.split(key, 6)
    slots_dev = SAMP_DEV * BAG
    devices = N_GRP * N_SHARD
    heavy = jax.random.randint(key_heavy, (devices,), 0, N_SHARD)
    positions = jax.vmap(lambda k: jax.random.permutation(k, slots_dev))(jax.random.split(key_perm, devices))
    others = (heavy[:, None] + 1 + (positions - FCAP) % (N_SHARD - 1)) % N_SHARD
    shard_of = jnp.where(positions < FCAP, heavy[:, None], others).reshape(SAMP, BAG)
    pick = jax.random.randint(key_pick, (SAMP, BAG), 0, 2)
    span = N_GRP * HOT_DEV
    left = jax.random.randint(key_left, (SAMP, BAG), 0, span)
    right = jax.random.randint(key_right, (SAMP, BAG), 0, span)
    skewed = left * right // span
    hot_id = (skewed // HOT_DEV * N_SHARD + shard_of) * HOT_DEV + skewed % HOT_DEV
    cold_id = shard_of * TR + jax.random.randint(key_cold, (SAMP, BAG), 0, TR)
    return jnp.where(pick == 1, hot_id, HOT + cold_id).astype(jnp.int32)


def draw_bag_len(key, part):
    key = jax.random.fold_in(key, 41)
    lengths = jax.random.randint(key, (SAMP,), 1, BAG + 1)
    first = jnp.arange(SAMP, dtype=jnp.int32) % SAMP_DEV == 0
    return jnp.where(first, BAG, lengths).astype(jnp.int32)


def levels(own_key, shape, shards, smallest, top_value):
    level, own = 1.0, jax.random.fold_in(own_key, 6)
    for position, blocks in shards:
        draws = jnp.exp(jax.random.uniform(jax.random.fold_in(own, position), (blocks,), jnp.float32, smallest / len(shards), top_value / len(shards)))
        level = level * jnp.repeat(draws, shape[position] // blocks).reshape([-1 if axis == position else 1 for axis in range(len(shape))])
    return level


def noise(key, shape, deviation, reach, cuts=(), kind=jnp.bfloat16):
    values = deviation * jax.random.normal(key, shape, jnp.float32)
    if cuts:
        values = values * levels(key, shape, cuts, -0.22, 0.18)
    return jnp.clip(values, -reach, reach).astype(kind)


def setup_inputs(seed: int = 0) -> dict:
    streams_of = jax.random.split(jax.random.key(seed), 6)
    return {
        "table": noise(streams_of[0], (ROWS, DIM), 1.0, 6.0, ((0, 768),), jnp.float32),
        "hot_offsets": draw_hot_offsets(jax.random.fold_in(streams_of[5], 71), 0),
        "cold_dest": draw_cold_dest(jax.random.fold_in(streams_of[5], 71), 0),
        "bag_ids": draw_bag_ids(jax.random.fold_in(streams_of[5], 71), 0),
        "bag_len": draw_bag_len(jax.random.fold_in(streams_of[5], 71), 0),
    }


def reference(table, hot_offsets, cold_dest, bag_ids, bag_len):
    owner = jnp.arange(HOT, dtype=jnp.int32) // HOT_DEV
    hot_abs = owner * TR + hot_offsets
    blocks = table.reshape(N_GRP, N_SHARD * NB, BLK, DIM)
    dest = cold_dest.reshape(N_GRP, N_SHARD * NB)
    base = jnp.arange(N_SHARD * NB, dtype=jnp.int32)

    def regroup(pair):
        group_blocks, group_dest = pair

        def per_dest(target):
            key_order = jnp.where(group_dest == target, base, N_SHARD * NB + base)
            picked = jnp.argsort(key_order)[:NB]
            return group_blocks[picked]

        return lax.map(per_dest, jnp.arange(N_SHARD, dtype=jnp.int32))

    new_table = lax.map(regroup, (blocks, dest)).reshape(ROWS, DIM)
    sample_group = jnp.arange(SAMP, dtype=jnp.int32) // SAMP_G
    is_hot = bag_ids < HOT
    hot_rows = hot_abs[jnp.clip(bag_ids, 0, HOT - 1)]
    cold_rows = sample_group[:, None] * ROWS_G + jnp.clip(bag_ids - HOT, 0, ROWS_G - 1)
    absolute = jnp.where(is_hot, hot_rows, cold_rows).astype(jnp.int32)
    live = jnp.arange(BAG, dtype=jnp.int32)[None, :] < bag_len[:, None]
    values = table[absolute] * live[:, :, None].astype(jnp.float32)
    pooled = jnp.sum(values, axis=1) / bag_len.astype(jnp.float32)[:, None]
    return new_table, pooled
```

```python
import functools

import jax
import jax.numpy as jnp
from jax import lax
from jax.experimental import pallas as pl
from jax.experimental.pallas import tpu as pltpu
from jax.sharding import PartitionSpec as P

MESH = pl.DeviceIdType.MESH
F32 = jnp.float32
BF16 = jnp.bfloat16
I32 = jnp.int32

NS = 24
NZ = 12
NB = 8
BLK = 64
W = 128
NBLK = NS * NB
SAMP = 32
BAG = 16
SLOTS = SAMP * BAG
HOTD = 16
ROWS = NB * BLK
GROUPS = NS // 4


def iota(shape, axis):
    return lax.broadcasted_iota(I32, shape, axis)


def onehot(mask):
    return jnp.where(mask, 1.0, 0.0).astype(BF16)


def nt(a, b):
    return lax.dot_general(a, b, (((1,), (1,)), ((), ())), preferred_element_type=F32)


def nn(a, b):
    return jnp.dot(a, b, preferred_element_type=F32)


def split2(x):
    hi = x.astype(BF16)
    return hi, (x - hi.astype(F32)).astype(BF16)


def first_row(m):
    return 8 * (m // 3) + 3 * lax.rem(m, 3)


def order(s):
    return lax.rem(s, 2) * NZ + s // 2


def wait_bytes(ref, sem):
    pltpu.make_async_copy(ref, ref, sem).wait()


def kernel(
    ng,
    table_h, off_h, dest_h, ids_h, len_h,
    moved, pooled,
    tbl, ids, off_s, dest_s, len_s,
    abuf, hl, hotloc, hotbuf, msg, req, xbuf, ybuf, cmat, pbuf, sbuf, pin, colv, keyv,
    load_sem, req_send, req_recv, hot_send, hot_recv, one_send, one_recv, two_send, two_recv,
    sib_send, sib_recv, sum_send, sum_recv,
):
    hotc = ng * HOTD
    cols = hotc + ROWS
    me = lax.axis_index("shard")
    grp = lax.axis_index("grp")
    core = lax.rem(me, 2)
    chip = me // 2
    sib = me + 1 - 2 * core
    mine = order(me)
    lane0 = lax.rem(mine, 4)
    three = lax.rem(me, 3) < 2

    loads = [
        pltpu.make_async_copy(table_h, tbl, load_sem.at[0]),
        pltpu.make_async_copy(ids_h, ids, load_sem.at[1]),
        pltpu.make_async_copy(len_h, len_s, load_sem.at[2]),
        pltpu.make_async_copy(off_h, off_s, load_sem.at[3]),
        pltpu.make_async_copy(dest_h, dest_s, load_sem.at[4]),
    ]
    for load in loads:
        load.start()

    barrier = pltpu.get_barrier_semaphore()

    @pl.loop(1, NS)
    def _(k):
        pl.semaphore_signal(
            barrier, inc=1, device_id={"shard": lax.rem(me + k, NS)}, device_id_type=MESH
        )

    @pl.loop(1, ng)
    def _(k):
        pl.semaphore_signal(
            barrier, inc=1, device_id={"grp": lax.rem(grp + k, ng)}, device_id_type=MESH
        )

    for load in loads[1:]:
        load.wait()

    lens = jnp.zeros((SAMP, W), I32)
    row = iota((SAMP, W), 0)
    for n in range(SAMP):
        lens = jnp.where(row == n, len_s[n], lens)
    bag = ids[...]
    hot_total = hotc * NS
    is_hot = bag < hot_total
    owner = bag >> 4
    turn = (owner * 43691) >> 20
    cold = jnp.maximum(bag - hot_total, 0)
    shard = jnp.where(is_hot, owner - turn * NS, cold >> 9)
    col = jnp.where(is_hot, turn * HOTD + (bag & (HOTD - 1)), hotc + (cold & (ROWS - 1)))
    live = iota((SAMP, BAG), 1) < lens[:, :BAG]
    shard = jnp.where(live, shard, 31)
    fields = jnp.concatenate([shard, col >> 5, col & 31], axis=0).astype(F32).astype(BF16)
    spread = nn(fields, onehot(iota((BAG, SLOTS), 0) == (iota((BAG, SLOTS), 1) & (BAG - 1))))
    own = iota((SAMP, SLOTS), 0) == (iota((SAMP, SLOTS), 1) >> 4)
    flat = [
        jnp.sum(jnp.where(own, spread[SAMP * i : SAMP * (i + 1)], 0.0), axis=0, keepdims=True)
        for i in range(3)
    ]
    to = jnp.where(flat[0] == iota((32, SLOTS), 0).astype(F32), 1.0, 0.0)
    to = jnp.where(iota((32, SLOTS), 0) < NS, to, 0.0)
    before = onehot(iota((SLOTS, SLOTS), 0) < iota((SLOTS, SLOTS), 1))
    rank = jnp.sum(to * nn(to.astype(BF16), before), axis=0, keepdims=True)
    place = onehot(
        rank.astype(I32) + 32 * lane0 == iota((W, SLOTS), 0)
    )
    sample1 = ((iota((1, SLOTS), 1) >> 4) + 1).astype(F32)
    packed = jnp.concatenate([to * flat[1], to * flat[2], to * sample1], axis=0).astype(BF16)
    placed = nt(packed, place)
    colpart = 32.0 * placed[0:NS] + placed[32 : 32 + NS]
    samppart = pltpu.roll(placed[64 : 64 + NS], 32, 1)
    dests = jnp.zeros((1, W), I32)
    lane = iota((1, W), 1)
    dlane = 32 * lax.rem(mine + 2, 4)
    for j in range(NB):
        dests = jnp.where(lane == dlane + j, dest_s[j], dests)
    msg[:, 0, :] = colpart + samppart + dests.astype(F32)

    loads[0].wait()
    hi, lo = split2(tbl[...])
    hl[hotc:cols, 0:W] = hi
    hl[hotc:cols, W : 2 * W] = lo
    offs = jnp.zeros((HOTD, ROWS), I32)
    hrow = iota((HOTD, ROWS), 0)
    for k in range(HOTD):
        offs = jnp.where(hrow == k, off_s[k], offs)
    picked = nn(onehot(offs == iota((HOTD, ROWS), 1)), hl[hotc:cols, :])
    hotloc[...] = picked[:, :W] + picked[:, W:]
    for r in range(BLK):
        abuf[r] = tbl[pl.ds(r, NB, stride=BLK), :]

    pl.semaphore_wait(barrier, NS - 1 + ng - 1)

    pltpu.make_async_copy(msg.at[pl.ds(me, 1)], req.at[pl.ds(mine, 1)], req_recv).start()

    @pl.loop(1, NS)
    def _(k):
        peer = lax.rem(me + k, NS)
        pltpu.make_async_remote_copy(
            src_ref=msg.at[pl.ds(peer, 1)], dst_ref=req.at[pl.ds(mine, 1)],
            send_sem=req_send, recv_sem=req_recv,
            device_id={"shard": peer}, device_id_type=MESH,
        ).start()

    hot_here = hotbuf.at[pl.ds(pl.multiple_of(grp * HOTD, HOTD), HOTD)]
    pltpu.make_async_copy(hotloc, hot_here, hot_recv).start()

    @pl.loop(1, ng)
    def _(k):
        pltpu.make_async_remote_copy(
            src_ref=hotloc, dst_ref=hot_here, send_sem=hot_send, recv_sem=hot_recv,
            device_id={"grp": lax.rem(grp + k, ng)}, device_id_type=MESH,
        ).start()

    def relay(peer, count, remote):
        src = abuf.at[pl.ds(first_row(peer), count)]
        dst = xbuf.at[0:count, pl.ds(pl.multiple_of(me * NB, NB), NB), :]
        if remote:
            pltpu.make_async_remote_copy(
                src_ref=src, dst_ref=dst, send_sem=one_send, recv_sem=one_recv,
                device_id={"shard": peer}, device_id_type=MESH,
            ).start()
        else:
            pltpu.make_async_copy(src, dst, one_recv).start()

    def by_count(peer, act):
        @pl.when(lax.rem(peer, 3) < 2)
        def _():
            act(3)

        @pl.when(lax.rem(peer, 3) == 2)
        def _():
            act(2)

    by_count(me, lambda count: relay(me, count, False))

    @pl.loop(1, NS)
    def _(k):
        peer = lax.rem(me + k, NS)
        by_count(peer, lambda count: relay(peer, count, True))

    wait_bytes(req, req_recv)
    asked = req[:, 0, :]
    who = iota((NS, W), 0)
    spot = (iota((NS, W), 1) >> 5) & 3
    first = jnp.where(spot == (who & 3), asked, 0.0)
    second = pltpu.roll(jnp.where(spot == ((who + 1) & 3), asked, 0.0), W - 32, 1)
    pad = jnp.zeros((8 - GROUPS, W), F32)
    gather4 = lambda x: jnp.concatenate(
        [jnp.sum(x[4 * g : 4 * g + 4], axis=0, keepdims=True) for g in range(GROUPS)] + [pad],
        axis=0,
    )
    colv[...] = gather4(first).astype(I32)
    samp = gather4(second).astype(I32)
    keyv[...] = jnp.where(samp > 0, samp - 1 + ((iota((8, W), 1) >> 5) << 5), -1)

    @pl.loop(0, GROUPS)
    def _(g):
        key = keyv[pl.ds(g, 1), :]
        want = colv[pl.ds(g, 1), :]
        sums = onehot(iota((W, W), 0) == key)
        names = onehot(iota((cols, W), 0) == want)
        cmat[pl.ds(pl.multiple_of(g * W, W), W), :] = nt(sums, names).astype(BF16)

    b = iota((W, NBLK), 1)
    bs = (((b >> 3) & 1) * NZ) + (b >> 4)
    dlanes = onehot(iota((W, NBLK), 0) == 32 * ((bs + 2) & 3) + (b & 7))
    bs24 = bs[0:NS]
    target = jnp.sum(
        jnp.where(iota((NS, NBLK), 0) == bs24, nn(asked.astype(BF16), dlanes), 0.0),
        axis=0, keepdims=True,
    ).astype(I32)
    goes = jnp.where(iota((32, NBLK), 0) == target, 1.0, 0.0)
    earlier = onehot(iota((NBLK, NBLK), 0) < iota((NBLK, NBLK), 1))
    seat = nn(goes.astype(BF16), earlier) + (NB * iota((32, NBLK), 0)).astype(F32)
    seat = jnp.sum(goes * seat, axis=0, keepdims=True).astype(I32)
    perm = onehot(iota((NBLK, NBLK), 0) == seat)

    wait_bytes(hotbuf, hot_recv)
    hi, lo = split2(hotbuf[...])
    hl[0:hotc, 0:W] = hi
    hl[0:hotc, W : 2 * W] = lo
    half = NZ * SAMP
    for h in range(2):
        part = nn(cmat[half * h : half * (h + 1), :], hl[...])
        pbuf[h] = (part[:, :W] + part[:, W:]).reshape(NZ, SAMP, W)
    to_sib = pltpu.make_async_remote_copy(
        src_ref=pbuf.at[1 - core], dst_ref=sbuf, send_sem=sib_send, recv_sem=sib_recv,
        device_id={"shard": sib}, device_id_type=MESH,
    )
    to_sib.start()

    @pl.when(three)
    def _():
        wait_bytes(xbuf, one_recv)

    @pl.when(jnp.logical_not(three))
    def _():
        wait_bytes(xbuf.at[0:2], one_recv)

    def reorder(i):
        x = xbuf[i]
        hi = x.astype(BF16)
        rest = x - hi.astype(F32)
        mid = rest.astype(BF16)
        low = (rest - mid.astype(F32)).astype(BF16)
        y = nn(perm, jnp.concatenate([hi, mid, low], axis=1))
        ybuf[i] = (y[:, :W] + y[:, W : 2 * W]) + y[:, 2 * W :]

    reorder(0)
    reorder(1)

    @pl.when(three)
    def _():
        reorder(2)

    def deliver(peer, count, remote):
        src = ybuf.at[0:count, pl.ds(pl.multiple_of(peer * NB, NB), NB), :]
        dst = moved.at[pl.ds(first_row(me), count)]
        if remote:
            pltpu.make_async_remote_copy(
                src_ref=src, dst_ref=dst, send_sem=two_send, recv_sem=two_recv,
                device_id={"shard": peer}, device_id_type=MESH,
            ).start()
        else:
            pltpu.make_async_copy(src, dst, two_recv).start()

    def deliver_all(count):
        deliver(me, count, False)

        @pl.loop(1, NS)
        def _(k):
            deliver(lax.rem(me + k, NS), count, True)

    by_count(me, deliver_all)

    to_sib.wait_recv()
    pbuf[core] += sbuf[...]
    pltpu.make_async_copy(pbuf.at[core, chip], pin.at[chip], sum_recv).start()

    @pl.loop(1, NZ)
    def _(k):
        z = lax.rem(chip + k, NZ)
        pltpu.make_async_remote_copy(
            src_ref=pbuf.at[core, z], dst_ref=pin.at[chip],
            send_sem=sum_send, recv_sem=sum_recv,
            device_id={"shard": 2 * z + core}, device_id_type=MESH,
        ).start()

    wait_bytes(pin, sum_recv)
    total = pin[0]
    for z in range(1, NZ):
        total += pin[z]
    pooled[...] = total / lens.astype(F32)

    wait_bytes(moved, two_recv)
    to_sib.wait_send()
    wait_bytes(req.at[0 : NS - 1], req_send)
    wait_bytes(hotbuf.at[0 : hotc - HOTD], hot_send)
    wait_bytes(pin.at[0 : NZ - 1], sum_send)

    @pl.when(three)
    def _():
        wait_bytes(abuf.at[0 : BLK - 3], one_send)
        wait_bytes(xbuf.at[:, 0 : NBLK - NB, :], two_send)

    @pl.when(jnp.logical_not(three))
    def _():
        wait_bytes(abuf.at[0 : BLK - 2], one_send)
        wait_bytes(xbuf.at[0:2, 0 : NBLK - NB, :], two_send)


def local(table, hot_offsets, cold_dest, bag_ids, bag_len):
    ng = lax.axis_size("grp")
    hotc = ng * HOTD
    cols = hotc + ROWS
    dma = pltpu.SemaphoreType.DMA
    moved, pooled = pl.pallas_call(
        functools.partial(kernel, ng),
        out_shape=(
            jax.ShapeDtypeStruct((BLK, NB, W), F32),
            jax.ShapeDtypeStruct((SAMP, W), F32),
        ),
        in_specs=[pl.BlockSpec(memory_space=pl.ANY)] * 5,
        out_specs=(
            pl.BlockSpec(memory_space=pl.ANY),
            pl.BlockSpec(memory_space=pltpu.VMEM),
        ),
        scratch_shapes=[
            pltpu.VMEM((ROWS, W), F32),
            pltpu.VMEM((SAMP, BAG), I32),
            pltpu.SMEM((HOTD,), I32),
            pltpu.SMEM((NB,), I32),
            pltpu.SMEM((SAMP,), I32),
            pltpu.VMEM((BLK, NB, W), F32),
            pltpu.VMEM((cols, 2 * W), BF16),
            pltpu.VMEM((HOTD, W), F32),
            pltpu.VMEM((hotc, W), F32),
            pltpu.VMEM((NS, 1, W), F32),
            pltpu.VMEM((NS, 1, W), F32),
            pltpu.VMEM((3, NBLK, W), F32),
            pltpu.VMEM((3, NBLK, W), F32),
            pltpu.VMEM((NS * SAMP, cols), BF16),
            pltpu.VMEM((2, NZ, SAMP, W), F32),
            pltpu.VMEM((NZ, SAMP, W), F32),
            pltpu.VMEM((NZ, SAMP, W), F32),
            pltpu.VMEM((8, W), I32),
            pltpu.VMEM((8, W), I32),
            dma((5,)),
        ]
        + [dma(())] * 12,
        compiler_params=pltpu.CompilerParams(
            collective_id=0, has_side_effects=True, vmem_limit_bytes=24 * 1024 * 1024
        ),
    )(table, hot_offsets, cold_dest, bag_ids, bag_len)
    return moved.transpose(1, 0, 2).reshape(ROWS, W), pooled


def solution(mesh):
    return jax.shard_map(
        local,
        mesh=mesh,
        in_specs=(
            P(("grp", "shard"), None),
            P(("grp", "shard")),
            P(("grp", "shard")),
            P(("grp", "shard"), None),
            P(("grp", "shard")),
        ),
        out_specs=(P(("grp", "shard"), None), P(("grp", "shard"), None)),
        check_vma=False,
    )
```

```python
import functools

import jax
import jax.numpy as jnp
from jax import lax
from jax.experimental import pallas as pl
from jax.experimental.pallas import tpu as pltpu
from jax.sharding import PartitionSpec as P

MESH = pl.DeviceIdType.MESH
F32 = jnp.float32
BF16 = jnp.bfloat16
I32 = jnp.int32

NS = 24
NZ = 12
HOP = 3
NB = 8
BLK = 64
W = 128
NBLK = NS * NB
SAMP = 32
BAG = 16
SLOTS = SAMP * BAG
HOTD = 16
ROWS = NB * BLK
GROUPS = NS // 4


def iota(shape, axis):
    return lax.broadcasted_iota(I32, shape, axis)


def onehot(mask):
    return jnp.where(mask, 1.0, 0.0).astype(BF16)


def nt(a, b):
    return lax.dot_general(a, b, (((1,), (1,)), ((), ())), preferred_element_type=F32)


def nn(a, b):
    return jnp.dot(a, b, preferred_element_type=F32)


def split2(x):
    hi = x.astype(BF16)
    return hi, (x - hi.astype(F32)).astype(BF16)


def first_row(m):
    return 8 * (m // 3) + 3 * lax.rem(m, 3)


def order(s):
    return lax.rem(s, 2) * NZ + s // 2


def far_first(me, n, act):
    act(lax.rem(me + n // 2, n))

    @pl.loop(1, n // 2)
    def _(q):
        act(lax.rem(me + n // 2 - q, n))
        act(lax.rem(me + n // 2 + q, n))


def wait_bytes(ref, sem):
    pltpu.make_async_copy(ref, ref, sem).wait()


def kernel(
    ng,
    table_h, off_h, dest_h, ids_h, len_h,
    moved, pooled,
    tbl, ids, off_s, dest_s, len_s,
    abuf, hl, hotloc, hotbuf, msg, req, xbuf, ybuf, cmat, pbuf, sbuf, rin, pin, colv, keyv,
    load_sem, req_send, req_recv, hot_send, hot_recv, one_send, one_recv, two_send, two_recv,
    sib_send, sib_recv, sum_send, sum_recv, far_recv,
):
    hotc = ng * HOTD
    cols = hotc + ROWS
    me = lax.axis_index("shard")
    grp = lax.axis_index("grp")
    core = lax.rem(me, 2)
    chip = me // 2
    sib = me + 1 - 2 * core
    mine = order(me)
    lane0 = lax.rem(mine, 4)
    three = lax.rem(me, 3) < 2

    loads = [
        pltpu.make_async_copy(table_h, tbl, load_sem.at[0]),
        pltpu.make_async_copy(ids_h, ids, load_sem.at[1]),
        pltpu.make_async_copy(len_h, len_s, load_sem.at[2]),
        pltpu.make_async_copy(off_h, off_s, load_sem.at[3]),
        pltpu.make_async_copy(dest_h, dest_s, load_sem.at[4]),
    ]
    for load in loads:
        load.start()

    barrier = pltpu.get_barrier_semaphore()

    def greet(where):
        pl.semaphore_signal(barrier, inc=1, device_id=where, device_id_type=MESH)

    far_first(me, NS, lambda peer: greet({"shard": peer}))
    far_first(grp, ng, lambda peer: greet({"grp": peer}))

    for load in loads[1:]:
        load.wait()

    lens = jnp.zeros((SAMP, W), I32)
    row = iota((SAMP, W), 0)
    for n in range(SAMP):
        lens = jnp.where(row == n, len_s[n], lens)
    bag = ids[...]
    hot_total = hotc * NS
    is_hot = bag < hot_total
    owner = bag >> 4
    turn = (owner * 43691) >> 20
    cold = jnp.maximum(bag - hot_total, 0)
    shard = jnp.where(is_hot, owner - turn * NS, cold >> 9)
    col = jnp.where(is_hot, turn * HOTD + (bag & (HOTD - 1)), hotc + (cold & (ROWS - 1)))
    square = iota((SAMP, SAMP), 0) == iota((SAMP, SAMP), 1)
    lens_row = jnp.sum(jnp.where(square, lens[:, :SAMP], 0), axis=0, keepdims=True)
    live = iota((BAG, SAMP), 0) < lens_row
    shard = jnp.where(live, shard, 31)
    fields = jnp.concatenate([shard, col >> 5, col & 31], axis=0).astype(F32).astype(BF16)
    spread = nn(fields, onehot(iota((SAMP, SLOTS), 0) == (iota((SAMP, SLOTS), 1) & (SAMP - 1))))
    own = iota((BAG, SLOTS), 0) == (iota((BAG, SLOTS), 1) >> 5)
    flat = [
        jnp.sum(jnp.where(own, spread[BAG * i : BAG * (i + 1)], 0.0), axis=0, keepdims=True)
        for i in range(3)
    ]
    to = jnp.where(flat[0] == iota((32, SLOTS), 0).astype(F32), 1.0, 0.0)
    to = jnp.where(iota((32, SLOTS), 0) < NS, to, 0.0)
    before = onehot(iota((SLOTS, SLOTS), 0) < iota((SLOTS, SLOTS), 1))
    rank = jnp.sum(to * nn(to.astype(BF16), before), axis=0, keepdims=True)
    place = onehot(
        rank.astype(I32) + 32 * lane0 == iota((W, SLOTS), 0)
    )
    sample1 = ((iota((1, SLOTS), 1) & (SAMP - 1)) + 1).astype(F32)
    packed = jnp.concatenate([to * flat[1], to * flat[2], to * sample1], axis=0).astype(BF16)
    placed = nt(packed, place)
    colpart = 32.0 * placed[0:NS] + placed[32 : 32 + NS]
    samppart = pltpu.roll(placed[64 : 64 + NS], 32, 1)
    dests = jnp.zeros((1, W), I32)
    lane = iota((1, W), 1)
    dlane = 32 * lax.rem(mine + 2, 4)
    for j in range(NB):
        dests = jnp.where(lane == dlane + j, dest_s[j], dests)
    msg[:, 0, :] = colpart + samppart + dests.astype(F32)

    loads[0].wait()
    hi, lo = split2(tbl[...])
    hl[hotc:cols, 0:W] = hi
    hl[hotc:cols, W : 2 * W] = lo
    offs = jnp.zeros((HOTD, ROWS), I32)
    hrow = iota((HOTD, ROWS), 0)
    for k in range(HOTD):
        offs = jnp.where(hrow == k, off_s[k], offs)
    picked = nn(onehot(offs == iota((HOTD, ROWS), 1)), hl[hotc:cols, :])
    hotloc[...] = picked[:, :W] + picked[:, W:]
    for r in range(BLK):
        abuf[r] = tbl[pl.ds(r, NB, stride=BLK), :]

    pl.semaphore_wait(barrier, NS - 1 + ng - 1)

    pltpu.make_async_copy(msg.at[pl.ds(me, 1)], req.at[pl.ds(mine, 1)], req_recv).start()

    far_first(me, NS, lambda peer: pltpu.make_async_remote_copy(
        src_ref=msg.at[pl.ds(peer, 1)], dst_ref=req.at[pl.ds(mine, 1)],
        send_sem=req_send, recv_sem=req_recv,
        device_id={"shard": peer}, device_id_type=MESH,
    ).start())

    hot_here = hotbuf.at[pl.ds(pl.multiple_of(grp * HOTD, HOTD), HOTD)]
    pltpu.make_async_copy(hotloc, hot_here, hot_recv).start()

    far_first(grp, ng, lambda peer: pltpu.make_async_remote_copy(
        src_ref=hotloc, dst_ref=hot_here, send_sem=hot_send, recv_sem=hot_recv,
        device_id={"grp": peer}, device_id_type=MESH,
    ).start())

    def push(src, dst, send_sem, recv_sem, peer):
        pltpu.make_async_remote_copy(
            src_ref=src, dst_ref=dst, send_sem=send_sem, recv_sem=recv_sem,
            device_id={"shard": peer}, device_id_type=MESH,
        ).start()

    def relay(peer, start, count):
        src = abuf.at[pl.ds(first_row(peer) + start, count)]
        dst = xbuf.at[
            start : start + count, pl.ds(pl.multiple_of(me * NB, NB), NB), :
        ]
        return src, dst

    def by_count(peer, act):
        @pl.when(lax.rem(peer, 3) < 2)
        def _():
            act(3)

        @pl.when(lax.rem(peer, 3) == 2)
        def _():
            act(2)

    pltpu.make_async_copy(*relay(me, 0, 1), one_recv.at[0]).start()
    by_count(
        me,
        lambda n: pltpu.make_async_copy(*relay(me, 1, n - 1), one_recv.at[1]).start(),
    )
    far_first(
        me, NS, lambda peer: push(*relay(peer, 0, 1), one_send, one_recv.at[0], peer)
    )
    far_first(me, NS, lambda peer: by_count(
        peer, lambda n: push(*relay(peer, 1, n - 1), one_send, one_recv.at[1], peer)
    ))

    wait_bytes(req, req_recv)
    asked = req[:, 0, :]
    b = iota((W, NBLK), 1)
    bs = (((b >> 3) & 1) * NZ) + (b >> 4)
    dlanes = onehot(iota((W, NBLK), 0) == 32 * ((bs + 2) & 3) + (b & 7))
    bs24 = bs[0:NS]
    target = jnp.sum(
        jnp.where(iota((NS, NBLK), 0) == bs24, nn(asked.astype(BF16), dlanes), 0.0),
        axis=0, keepdims=True,
    ).astype(I32)
    goes = jnp.where(iota((32, NBLK), 0) == target, 1.0, 0.0)
    earlier = onehot(iota((NBLK, NBLK), 0) < iota((NBLK, NBLK), 1))
    seat = nn(goes.astype(BF16), earlier) + (NB * iota((32, NBLK), 0)).astype(F32)
    seat = jnp.sum(goes * seat, axis=0, keepdims=True).astype(I32)
    perm = onehot(iota((NBLK, NBLK), 0) == seat)

    def reorder(i):
        x = xbuf[i]
        hi = x.astype(BF16)
        rest = x - hi.astype(F32)
        mid = rest.astype(BF16)
        low = (rest - mid.astype(F32)).astype(BF16)
        y = nn(perm, jnp.concatenate([hi, mid, low], axis=1))
        ybuf[i] = (y[:, :W] + y[:, W : 2 * W]) + y[:, 2 * W :]

    def deliver(peer, start, count):
        src = ybuf.at[
            start : start + count, pl.ds(pl.multiple_of(peer * NB, NB), NB), :
        ]
        return src, moved.at[pl.ds(first_row(me) + start, count)]

    def deliver_all(start, count):
        pltpu.make_async_copy(*deliver(me, start, count), two_recv).start()
        far_first(
            me, NS,
            lambda peer: push(*deliver(peer, start, count), two_send, two_recv, peer),
        )

    wait_bytes(xbuf.at[0:1], one_recv.at[0])
    reorder(0)
    deliver_all(0, 1)

    who = iota((NS, W), 0)
    spot = (iota((NS, W), 1) >> 5) & 3
    first = jnp.where(spot == (who & 3), asked, 0.0)
    second = pltpu.roll(jnp.where(spot == ((who + 1) & 3), asked, 0.0), W - 32, 1)
    pad = jnp.zeros((8 - GROUPS, W), F32)
    gather4 = lambda x: jnp.concatenate(
        [jnp.sum(x[4 * g : 4 * g + 4], axis=0, keepdims=True) for g in range(GROUPS)] + [pad],
        axis=0,
    )
    colv[...] = gather4(first).astype(I32)
    samp = gather4(second).astype(I32)
    keyv[...] = jnp.where(samp > 0, samp - 1 + ((iota((8, W), 1) >> 5) << 5), -1)

    @pl.loop(0, GROUPS)
    def _(g):
        key = keyv[pl.ds(g, 1), :]
        want = colv[pl.ds(g, 1), :]
        sums = onehot(iota((W, W), 0) == key)
        names = onehot(iota((cols, W), 0) == want)
        cmat[pl.ds(pl.multiple_of(g * W, W), W), :] = nt(sums, names).astype(BF16)

    wait_bytes(hotbuf, hot_recv)
    hi, lo = split2(hotbuf[...])
    hl[0:hotc, 0:W] = hi
    hl[0:hotc, W : 2 * W] = lo
    half = NZ * SAMP
    for h in range(2):
        part = nn(cmat[half * h : half * (h + 1), :], hl[...])
        pbuf[h] = (part[:, :W] + part[:, W:]).reshape(NZ, SAMP, W)
    to_sib = pltpu.make_async_remote_copy(
        src_ref=pbuf.at[1 - core], dst_ref=sbuf, send_sem=sib_send, recv_sem=sib_recv,
        device_id={"shard": sib}, device_id_type=MESH,
    )
    to_sib.start()
    to_sib.wait_recv()
    pbuf[core] += sbuf[...]
    pltpu.make_async_copy(pbuf.at[core, chip], pin.at[HOP], sum_recv).start()

    def chip_at(step):
        return lax.rem(chip + step + NZ, NZ)

    def send_sum(step, via, dst, recv_sem):
        push(
            pbuf.at[core, chip_at(step)], dst, sum_send, recv_sem,
            2 * chip_at(via) + core,
        )

    send_sum(6, 3 + 6 * core, rin.at[4], far_recv)
    for i, step in enumerate((-5, 5, -4, 4)):
        send_sum(step, step - HOP if step > 0 else step + HOP, rin.at[i], far_recv)
    for step in (-2, 2, -1, 1):
        send_sum(step, step, pin.at[HOP + step], sum_recv)

    by_count(me, lambda n: wait_bytes(xbuf.at[1:n], one_recv.at[1]))
    reorder(1)

    @pl.when(three)
    def _():
        reorder(2)

    by_count(me, lambda n: deliver_all(1, n - 1))

    wait_bytes(rin, far_recv)
    pbuf[core, chip_at(-HOP)] += rin[0] + rin[2]
    pbuf[core, chip_at(HOP)] += rin[1] + rin[3]
    pbuf[core, chip_at(HOP + 6 * core)] += rin[4]
    for step in (-HOP, HOP):
        send_sum(step, step, pin.at[HOP + step], sum_recv)
    wait_bytes(pin, sum_recv)
    total = pin[0]
    for z in range(1, 2 * HOP + 1):
        total += pin[z]
    pooled[...] = total / lens.astype(F32)

    wait_bytes(moved, two_recv)
    to_sib.wait_send()
    wait_bytes(req.at[0 : NS - 1], req_send)
    wait_bytes(hotbuf.at[0 : hotc - HOTD], hot_send)
    wait_bytes(pbuf.at[0, 0 : NZ - 1], sum_send)

    by_count(me, lambda n: wait_bytes(abuf.at[0 : BLK - n], one_send))
    by_count(me, lambda n: wait_bytes(xbuf.at[0:n, 0 : NBLK - NB, :], two_send))


def local(table, hot_offsets, cold_dest, bag_ids, bag_len):
    ng = lax.axis_size("grp")
    hotc = ng * HOTD
    cols = hotc + ROWS
    dma = pltpu.SemaphoreType.DMA
    moved, pooled = pl.pallas_call(
        functools.partial(kernel, ng),
        out_shape=(
            jax.ShapeDtypeStruct((BLK, NB, W), F32),
            jax.ShapeDtypeStruct((SAMP, W), F32),
        ),
        in_specs=[pl.BlockSpec(memory_space=pltpu.HBM)] * 5,
        out_specs=(
            pl.BlockSpec(memory_space=pl.ANY),
            pl.BlockSpec(memory_space=pltpu.VMEM),
        ),
        scratch_shapes=[
            pltpu.VMEM((ROWS, W), F32),
            pltpu.VMEM((BAG, SAMP), I32),
            pltpu.SMEM((HOTD,), I32),
            pltpu.SMEM((NB,), I32),
            pltpu.SMEM((SAMP,), I32),
            pltpu.VMEM((BLK, NB, W), F32),
            pltpu.VMEM((cols, 2 * W), BF16),
            pltpu.VMEM((HOTD, W), F32),
            pltpu.VMEM((hotc, W), F32),
            pltpu.VMEM((NS, 1, W), F32),
            pltpu.VMEM((NS, 1, W), F32),
            pltpu.VMEM((3, NBLK, W), F32),
            pltpu.VMEM((3, NBLK, W), F32),
            pltpu.VMEM((NS * SAMP, cols), BF16),
            pltpu.VMEM((2, NZ, SAMP, W), F32),
            pltpu.VMEM((NZ, SAMP, W), F32),
            pltpu.VMEM((5, SAMP, W), F32),
            pltpu.VMEM((2 * HOP + 1, SAMP, W), F32),
            pltpu.VMEM((8, W), I32),
            pltpu.VMEM((8, W), I32),
            dma((5,)),
        ]
        + [dma(())] * 5
        + [dma((2,))]
        + [dma(())] * 7,
        compiler_params=pltpu.CompilerParams(
            collective_id=0, has_side_effects=True, vmem_limit_bytes=24 * 1024 * 1024
        ),
    )(
        *(
            pltpu.with_memory_space_constraint(x, pltpu.HBM)
            for x in (table, hot_offsets, cold_dest, bag_ids.T, bag_len)
        )
    )
    return moved.transpose(1, 0, 2).reshape(ROWS, W), pooled


def solution(mesh):
    return jax.shard_map(
        local,
        mesh=mesh,
        in_specs=(
            P(("grp", "shard"), None),
            P(("grp", "shard")),
            P(("grp", "shard")),
            P(("grp", "shard"), None),
            P(("grp", "shard")),
        ),
        out_specs=(P(("grp", "shard"), None), P(("grp", "shard"), None)),
        check_vma=False,
    )
```

```python
import functools

import jax
import jax.numpy as jnp
from jax import lax
from jax.experimental import pallas as pl
from jax.experimental.pallas import tpu as pltpu
from jax.sharding import PartitionSpec as P

MESH = pl.DeviceIdType.MESH
F32 = jnp.float32
BF16 = jnp.bfloat16
I32 = jnp.int32

NS = 24
NZ = 12
HOP = 3
NB = 8
BLK = 64
W = 128
NBLK = NS * NB
SAMP = 32
BAG = 16
SLOTS = SAMP * BAG
HOTD = 16
ROWS = NB * BLK
GROUPS = NS // 4


def iota(shape, axis):
    return lax.broadcasted_iota(I32, shape, axis)


def onehot(mask):
    return jnp.where(mask, 1.0, 0.0).astype(BF16)


def nt(a, b):
    return lax.dot_general(a, b, (((1,), (1,)), ((), ())), preferred_element_type=F32)


def nn(a, b):
    return jnp.dot(a, b, preferred_element_type=F32)


def split2(x):
    hi = x.astype(BF16)
    return hi, (x - hi.astype(F32)).astype(BF16)


def first_row(m):
    return 8 * (m // 3) + 3 * lax.rem(m, 3)


def order(s):
    return lax.rem(s, 2) * NZ + s // 2


def far_first(me, n, act):
    act(lax.rem(me + n // 2, n))

    @pl.loop(1, n // 2)
    def _(q):
        act(lax.rem(me + n // 2 - q, n))
        act(lax.rem(me + n // 2 + q, n))


def wait_bytes(ref, sem):
    pltpu.make_async_copy(ref, ref, sem).wait()


def kernel(
    ng,
    table_h, off_h, dest_h, ids_h, len_h,
    moved, pooled,
    tbl, ids, off_s, dest_s, len_s,
    abuf, hl, hotloc, hotbuf, msg, req, xbuf, ybuf, cmat, pbuf, sbuf, rin, pin, colv, keyv,
    load_sem, req_send, req_recv, hot_send, hot_recv, one_send, one_recv, two_send, two_recv,
    sib_send, sib_recv, sum_send, sum_recv, far_recv,
    column_sem, plane_sem,
):
    hotc = ng * HOTD
    cols = hotc + ROWS
    me = lax.axis_index("shard")
    grp = lax.axis_index("grp")
    core = lax.rem(me, 2)
    chip = me // 2
    sib = me + 1 - 2 * core
    mine = order(me)
    lane0 = lax.rem(mine, 4)
    three = lax.rem(me, 3) < 2

    barrier = pltpu.get_barrier_semaphore()

    def greet(where):
        pl.semaphore_signal(barrier, inc=1, device_id=where, device_id_type=MESH)

    far_first(chip, NZ, lambda z: greet({"shard": 2 * z}))
    far_first(grp, ng, lambda g: greet({"grp": g, "shard": 2 * chip + 1}))
    greet({"shard": sib})

    loads = [
        pltpu.make_async_copy(table_h, tbl, load_sem.at[0]),
        pltpu.make_async_copy(ids_h, ids, load_sem.at[1]),
        pltpu.make_async_copy(len_h, len_s, load_sem.at[2]),
        pltpu.make_async_copy(off_h, off_s, load_sem.at[3]),
        pltpu.make_async_copy(dest_h, dest_s, load_sem.at[4]),
    ]
    for load in loads:
        load.start()

    for load in loads[1:]:
        load.wait()

    lens = jnp.zeros((SAMP, W), I32)
    row = iota((SAMP, W), 0)
    for n in range(SAMP):
        lens = jnp.where(row == n, len_s[n], lens)
    bag = ids[...]
    hot_total = hotc * NS
    is_hot = bag < hot_total
    owner = bag >> 4
    turn = (owner * 43691) >> 20
    cold = jnp.maximum(bag - hot_total, 0)
    shard = jnp.where(is_hot, owner - turn * NS, cold >> 9)
    col = jnp.where(is_hot, turn * HOTD + (bag & (HOTD - 1)), hotc + (cold & (ROWS - 1)))
    square = iota((SAMP, SAMP), 0) == iota((SAMP, SAMP), 1)
    lens_row = jnp.sum(jnp.where(square, lens[:, :SAMP], 0), axis=0, keepdims=True)
    live = iota((BAG, SAMP), 0) < lens_row
    shard = jnp.where(live, shard, 31)
    fields = jnp.concatenate([shard, col >> 5, col & 31], axis=0).astype(F32).astype(BF16)
    spread = nn(fields, onehot(iota((SAMP, SLOTS), 0) == (iota((SAMP, SLOTS), 1) & (SAMP - 1))))
    own = iota((BAG, SLOTS), 0) == (iota((BAG, SLOTS), 1) >> 5)
    flat = [
        jnp.sum(jnp.where(own, spread[BAG * i : BAG * (i + 1)], 0.0), axis=0, keepdims=True)
        for i in range(3)
    ]
    to = jnp.where(flat[0] == iota((32, SLOTS), 0).astype(F32), 1.0, 0.0)
    to = jnp.where(iota((32, SLOTS), 0) < NS, to, 0.0)
    before = onehot(iota((SLOTS, SLOTS), 0) < iota((SLOTS, SLOTS), 1))
    rank = jnp.sum(to * nn(to.astype(BF16), before), axis=0, keepdims=True)
    place = onehot(
        rank.astype(I32) + 32 * lane0 == iota((W, SLOTS), 0)
    )
    sample1 = ((iota((1, SLOTS), 1) & (SAMP - 1)) + 1).astype(F32)
    packed = jnp.concatenate([to * flat[1], to * flat[2], to * sample1], axis=0).astype(BF16)
    placed = nt(packed, place)
    colpart = 32.0 * placed[0:NS] + placed[32 : 32 + NS]
    samppart = pltpu.roll(placed[64 : 64 + NS], 32, 1)
    dests = jnp.zeros((1, W), I32)
    lane = iota((1, W), 1)
    dlane = 32 * lax.rem(mine + 2, 4)
    for j in range(NB):
        dests = jnp.where(lane == dlane + j, dest_s[j], dests)
    msg[:, 0, :] = colpart + samppart + dests.astype(F32)

    loads[0].wait()
    hi, lo = split2(tbl[...])
    hl[hotc:cols, 0:W] = hi
    hl[hotc:cols, W : 2 * W] = lo
    offs = jnp.zeros((HOTD, ROWS), I32)
    hrow = iota((HOTD, ROWS), 0)
    for k in range(HOTD):
        offs = jnp.where(hrow == k, off_s[k], offs)
    picked = nn(onehot(offs == iota((HOTD, ROWS), 1)), hl[hotc:cols, :])
    hotloc[...] = picked[:, :W] + picked[:, W:]
    for r in range(BLK):
        abuf[r] = tbl[pl.ds(r, NB, stride=BLK), :]

    def tell(sem):
        pl.semaphore_signal(sem, inc=1, device_id={"shard": sib}, device_id_type=MESH)

    @pl.when(core == 0)
    def _():
        pl.semaphore_wait(barrier, NS - 1)
        tell(column_sem)

    @pl.when(core == 1)
    def _():
        pl.semaphore_wait(column_sem, 1)

    pltpu.make_async_copy(msg.at[pl.ds(me, 1)], req.at[pl.ds(mine, 1)], req_recv).start()

    far_first(me, NS, lambda peer: pltpu.make_async_remote_copy(
        src_ref=msg.at[pl.ds(peer, 1)], dst_ref=req.at[pl.ds(mine, 1)],
        send_sem=req_send, recv_sem=req_recv,
        device_id={"shard": peer}, device_id_type=MESH,
    ).start())

    def push(src, dst, send_sem, recv_sem, peer):
        pltpu.make_async_remote_copy(
            src_ref=src, dst_ref=dst, send_sem=send_sem, recv_sem=recv_sem,
            device_id={"shard": peer}, device_id_type=MESH,
        ).start()

    def relay(peer, start, count):
        src = abuf.at[pl.ds(first_row(peer) + start, count)]
        dst = xbuf.at[
            start : start + count, pl.ds(pl.multiple_of(me * NB, NB), NB), :
        ]
        return src, dst

    def by_count(peer, act):
        @pl.when(lax.rem(peer, 3) < 2)
        def _():
            act(3)

        @pl.when(lax.rem(peer, 3) == 2)
        def _():
            act(2)

    pltpu.make_async_copy(*relay(me, 0, 1), one_recv.at[0]).start()
    by_count(
        me,
        lambda n: pltpu.make_async_copy(*relay(me, 1, n - 1), one_recv.at[1]).start(),
    )
    far_first(
        me, NS, lambda peer: push(*relay(peer, 0, 1), one_send, one_recv.at[0], peer)
    )
    far_first(me, NS, lambda peer: by_count(
        peer, lambda n: push(*relay(peer, 1, n - 1), one_send, one_recv.at[1], peer)
    ))

    @pl.when(core == 1)
    def _():
        pl.semaphore_wait(barrier, 2 * ng - 1)
        tell(plane_sem)

    @pl.when(core == 0)
    def _():
        pl.semaphore_wait(plane_sem, 1)

    hot_here = hotbuf.at[pl.ds(pl.multiple_of(grp * HOTD, HOTD), HOTD)]
    pltpu.make_async_copy(hotloc, hot_here, hot_recv).start()

    far_first(grp, ng, lambda peer: pltpu.make_async_remote_copy(
        src_ref=hotloc, dst_ref=hot_here, send_sem=hot_send, recv_sem=hot_recv,
        device_id={"grp": peer}, device_id_type=MESH,
    ).start())

    wait_bytes(req, req_recv)
    asked = req[:, 0, :]
    b = iota((W, NBLK), 1)
    bs = (((b >> 3) & 1) * NZ) + (b >> 4)
    dlanes = onehot(iota((W, NBLK), 0) == 32 * ((bs + 2) & 3) + (b & 7))
    bs24 = bs[0:NS]
    target = jnp.sum(
        jnp.where(iota((NS, NBLK), 0) == bs24, nn(asked.astype(BF16), dlanes), 0.0),
        axis=0, keepdims=True,
    ).astype(I32)
    goes = jnp.where(iota((32, NBLK), 0) == target, 1.0, 0.0)
    earlier = onehot(iota((NBLK, NBLK), 0) < iota((NBLK, NBLK), 1))
    seat = nn(goes.astype(BF16), earlier) + (NB * iota((32, NBLK), 0)).astype(F32)
    seat = jnp.sum(goes * seat, axis=0, keepdims=True).astype(I32)
    perm = onehot(iota((NBLK, NBLK), 0) == seat)

    def reorder(i):
        x = xbuf[i]
        hi = x.astype(BF16)
        rest = x - hi.astype(F32)
        mid = rest.astype(BF16)
        low = (rest - mid.astype(F32)).astype(BF16)
        y = nn(perm, jnp.concatenate([hi, mid, low], axis=1))
        ybuf[i] = (y[:, :W] + y[:, W : 2 * W]) + y[:, 2 * W :]

    def deliver(peer, start, count):
        src = ybuf.at[
            start : start + count, pl.ds(pl.multiple_of(peer * NB, NB), NB), :
        ]
        return src, moved.at[pl.ds(first_row(me) + start, count)]

    def deliver_all(start, count):
        pltpu.make_async_copy(*deliver(me, start, count), two_recv).start()
        far_first(
            me, NS,
            lambda peer: push(*deliver(peer, start, count), two_send, two_recv, peer),
        )

    who = iota((NS, W), 0)
    spot = (iota((NS, W), 1) >> 5) & 3
    first = jnp.where(spot == (who & 3), asked, 0.0)
    second = pltpu.roll(jnp.where(spot == ((who + 1) & 3), asked, 0.0), W - 32, 1)
    pad = jnp.zeros((8 - GROUPS, W), F32)
    gather4 = lambda x: jnp.concatenate(
        [jnp.sum(x[4 * g : 4 * g + 4], axis=0, keepdims=True) for g in range(GROUPS)] + [pad],
        axis=0,
    )
    colv[...] = gather4(first).astype(I32)
    samp = gather4(second).astype(I32)
    keyv[...] = jnp.where(samp > 0, samp - 1 + ((iota((8, W), 1) >> 5) << 5), -1)

    @pl.loop(0, GROUPS)
    def _(g):
        key = keyv[pl.ds(g, 1), :]
        want = colv[pl.ds(g, 1), :]
        sums = onehot(iota((W, W), 0) == key)
        names = onehot(iota((cols, W), 0) == want)
        cmat[pl.ds(pl.multiple_of(g * W, W), W), :] = nt(sums, names).astype(BF16)

    wait_bytes(xbuf.at[0:1], one_recv.at[0])
    reorder(0)
    deliver_all(0, 1)

    wait_bytes(hotbuf, hot_recv)
    hi, lo = split2(hotbuf[...])
    hl[0:hotc, 0:W] = hi
    hl[0:hotc, W : 2 * W] = lo
    half = NZ * SAMP
    for h in range(2):
        part = nn(cmat[half * h : half * (h + 1), :], hl[...])
        pbuf[h] = (part[:, :W] + part[:, W:]).reshape(NZ, SAMP, W)
    to_sib = pltpu.make_async_remote_copy(
        src_ref=pbuf.at[1 - core], dst_ref=sbuf, send_sem=sib_send, recv_sem=sib_recv,
        device_id={"shard": sib}, device_id_type=MESH,
    )
    to_sib.start()
    to_sib.wait_recv()
    pbuf[core] += sbuf[...]
    pltpu.make_async_copy(pbuf.at[core, chip], pin.at[HOP], sum_recv).start()

    def chip_at(step):
        return lax.rem(chip + step + NZ, NZ)

    def send_sum(step, via, dst, recv_sem):
        push(
            pbuf.at[core, chip_at(step)], dst, sum_send, recv_sem,
            2 * chip_at(via) + core,
        )

    send_sum(6, 3 + 6 * core, rin.at[4], far_recv)
    for i, step in enumerate((-5, 5, -4, 4)):
        send_sum(step, step - HOP if step > 0 else step + HOP, rin.at[i], far_recv)
    for step in (-2, 2, -1, 1):
        send_sum(step, step, pin.at[HOP + step], sum_recv)

    by_count(me, lambda n: wait_bytes(xbuf.at[1:n], one_recv.at[1]))
    reorder(1)

    @pl.when(three)
    def _():
        reorder(2)

    by_count(me, lambda n: deliver_all(1, n - 1))

    wait_bytes(rin, far_recv)
    pbuf[core, chip_at(-HOP)] += rin[0] + rin[2]
    pbuf[core, chip_at(HOP)] += rin[1] + rin[3]
    pbuf[core, chip_at(HOP + 6 * core)] += rin[4]
    for step in (-HOP, HOP):
        send_sum(step, step, pin.at[HOP + step], sum_recv)
    wait_bytes(pin, sum_recv)
    total = pin[0]
    for z in range(1, 2 * HOP + 1):
        total += pin[z]
    pooled[...] = total / lens.astype(F32)

    wait_bytes(moved, two_recv)
    to_sib.wait_send()
    wait_bytes(req.at[0 : NS - 1], req_send)
    wait_bytes(hotbuf.at[0 : hotc - HOTD], hot_send)
    wait_bytes(pbuf.at[0, 0 : NZ - 1], sum_send)

    by_count(me, lambda n: wait_bytes(abuf.at[0 : BLK - n], one_send))
    by_count(me, lambda n: wait_bytes(xbuf.at[0:n, 0 : NBLK - NB, :], two_send))


def finish(moved, sums, table, pooled):
    for r in range(BLK):
        table[pl.ds(r, NB, stride=BLK), :] = moved[r]
    pooled[...] = sums[...]


def local(table, hot_offsets, cold_dest, bag_ids, bag_len):
    ng = lax.axis_size("grp")
    hotc = ng * HOTD
    cols = hotc + ROWS
    dma = pltpu.SemaphoreType.DMA
    moved, pooled = pl.pallas_call(
        functools.partial(kernel, ng),
        out_shape=(
            jax.ShapeDtypeStruct((BLK, NB, W), F32),
            jax.ShapeDtypeStruct((SAMP, W), F32),
        ),
        in_specs=[pl.BlockSpec(memory_space=pltpu.HBM)] * 5,
        out_specs=(
            pl.BlockSpec(memory_space=pl.ANY),
            pl.BlockSpec(memory_space=pltpu.VMEM),
        ),
        scratch_shapes=[
            pltpu.VMEM((ROWS, W), F32),
            pltpu.VMEM((BAG, SAMP), I32),
            pltpu.SMEM((HOTD,), I32),
            pltpu.SMEM((NB,), I32),
            pltpu.SMEM((SAMP,), I32),
            pltpu.VMEM((BLK, NB, W), F32),
            pltpu.VMEM((cols, 2 * W), BF16),
            pltpu.VMEM((HOTD, W), F32),
            pltpu.VMEM((hotc, W), F32),
            pltpu.VMEM((NS, 1, W), F32),
            pltpu.VMEM((NS, 1, W), F32),
            pltpu.VMEM((3, NBLK, W), F32),
            pltpu.VMEM((3, NBLK, W), F32),
            pltpu.VMEM((NS * SAMP, cols), BF16),
            pltpu.VMEM((2, NZ, SAMP, W), F32),
            pltpu.VMEM((NZ, SAMP, W), F32),
            pltpu.VMEM((5, SAMP, W), F32),
            pltpu.VMEM((2 * HOP + 1, SAMP, W), F32),
            pltpu.VMEM((8, W), I32),
            pltpu.VMEM((8, W), I32),
            dma((5,)),
        ]
        + [dma(())] * 5
        + [dma((2,))]
        + [dma(())] * 7
        + [pltpu.SemaphoreType.REGULAR] * 2,
        compiler_params=pltpu.CompilerParams(
            collective_id=0, has_side_effects=True, vmem_limit_bytes=24 * 1024 * 1024
        ),
    )(
        *(
            pltpu.with_memory_space_constraint(x, pltpu.HBM)
            for x in (table, hot_offsets, cold_dest, bag_ids.T, bag_len)
        )
    )
    return pl.pallas_call(
        finish,
        out_shape=(
            jax.ShapeDtypeStruct((ROWS, W), F32),
            jax.ShapeDtypeStruct((SAMP, W), F32),
        ),
        in_specs=[pl.BlockSpec(memory_space=pltpu.VMEM)] * 2,
        out_specs=[pl.BlockSpec(memory_space=pltpu.VMEM)] * 2,
    )(
        pltpu.with_memory_space_constraint(moved, pltpu.VMEM),
        pltpu.with_memory_space_constraint(pooled, pltpu.VMEM),
    )


def solution(mesh):
    return jax.shard_map(
        local,
        mesh=mesh,
        in_specs=(
            P(("grp", "shard"), None),
            P(("grp", "shard")),
            P(("grp", "shard")),
            P(("grp", "shard"), None),
            P(("grp", "shard")),
        ),
        out_specs=(P(("grp", "shard"), None), P(("grp", "shard"), None)),
        check_vma=False,
    )
```

```python
import functools

import jax
import jax.numpy as jnp
from jax import lax
from jax.experimental import pallas as pl
from jax.experimental.pallas import tpu as pltpu
from jax.sharding import PartitionSpec as P

MESH = pl.DeviceIdType.MESH
F32 = jnp.float32
BF16 = jnp.bfloat16
I32 = jnp.int32

NS = 24
NZ = 12
HOP = 3
NB = 8
BLK = 64
W = 128
NBLK = NS * NB
SAMP = 32
BAG = 16
SLOTS = SAMP * BAG
HOTD = 16
ROWS = NB * BLK
GROUPS = NS // 4


def iota(shape, axis):
    return lax.broadcasted_iota(I32, shape, axis)


def onehot(mask):
    return jnp.where(mask, 1.0, 0.0).astype(BF16)


def nt(a, b):
    return lax.dot_general(a, b, (((1,), (1,)), ((), ())), preferred_element_type=F32)


def nn(a, b):
    return jnp.dot(a, b, preferred_element_type=F32)


def split2(x):
    hi = x.astype(BF16)
    return hi, (x - hi.astype(F32)).astype(BF16)


def first_row(m):
    return 8 * (m // 3) + 3 * lax.rem(m, 3)


def order(s):
    return lax.rem(s, 2) * NZ + s // 2


def far_first(me, n, act):
    act(lax.rem(me + n // 2, n))

    @pl.loop(1, n // 2)
    def _(q):
        act(lax.rem(me + n // 2 - q, n))
        act(lax.rem(me + n // 2 + q, n))


def wait_bytes(ref, sem):
    pltpu.make_async_copy(ref, ref, sem).wait()


def kernel(
    ng,
    table_h, off_h, dest_h, ids_h, len_h,
    moved, pooled,
    tbl, ids, off_s, dest_s, len_s,
    abuf, hl, hotloc, hotbuf, msg, req, xbuf, ybuf, cmat, pbuf, sbuf, rin, pin, colv, keyv,
    load_sem, req_send, req_recv, hot_send, hot_recv, one_send, one_recv, two_send, two_recv,
    sib_send, sib_recv, sum_send, sum_recv, far_recv,
    column_sem, plane_sem,
):
    hotc = ng * HOTD
    cols = hotc + ROWS
    me = lax.axis_index("shard")
    grp = lax.axis_index("grp")
    core = lax.rem(me, 2)
    chip = me // 2
    sib = me + 1 - 2 * core
    mine = order(me)
    lane0 = lax.rem(mine, 4)
    three = lax.rem(me, 3) < 2

    barrier = pltpu.get_barrier_semaphore()

    def greet(where):
        pl.semaphore_signal(barrier, inc=1, device_id=where, device_id_type=MESH)

    far_first(chip, NZ, lambda z: greet({"shard": 2 * z}))
    far_first(grp, ng, lambda g: greet({"grp": g, "shard": 2 * chip + 1}))
    greet({"shard": sib})

    loads = [
        pltpu.make_async_copy(table_h, tbl, load_sem.at[0]),
        pltpu.make_async_copy(ids_h, ids, load_sem.at[1]),
        pltpu.make_async_copy(len_h, len_s, load_sem.at[2]),
        pltpu.make_async_copy(off_h, off_s, load_sem.at[3]),
        pltpu.make_async_copy(dest_h, dest_s, load_sem.at[4]),
    ]
    for load in loads:
        load.start()

    for load in loads[1:]:
        load.wait()

    lens = jnp.zeros((SAMP, W), I32)
    row = iota((SAMP, W), 0)
    for n in range(SAMP):
        lens = jnp.where(row == n, len_s[n], lens)
    bag = ids[...]
    hot_total = hotc * NS
    is_hot = bag < hot_total
    owner = bag >> 4
    turn = (owner * 43691) >> 20
    cold = jnp.maximum(bag - hot_total, 0)
    shard = jnp.where(is_hot, owner - turn * NS, cold >> 9)
    col = jnp.where(is_hot, turn * HOTD + (bag & (HOTD - 1)), hotc + (cold & (ROWS - 1)))
    square = iota((SAMP, SAMP), 0) == iota((SAMP, SAMP), 1)
    lens_row = jnp.sum(jnp.where(square, lens[:, :SAMP], 0), axis=0, keepdims=True)
    live = iota((BAG, SAMP), 0) < lens_row
    shard = jnp.where(live, shard, 31)
    fields = jnp.concatenate([shard, col >> 5, col & 31], axis=0).astype(F32).astype(BF16)
    spread = nn(fields, onehot(iota((SAMP, SLOTS), 0) == (iota((SAMP, SLOTS), 1) & (SAMP - 1))))
    own = iota((BAG, SLOTS), 0) == (iota((BAG, SLOTS), 1) >> 5)
    flat = [
        jnp.sum(jnp.where(own, spread[BAG * i : BAG * (i + 1)], 0.0), axis=0, keepdims=True)
        for i in range(3)
    ]
    to = jnp.where(flat[0] == iota((32, SLOTS), 0).astype(F32), 1.0, 0.0)
    to = jnp.where(iota((32, SLOTS), 0) < NS, to, 0.0)
    before = onehot(iota((SLOTS, SLOTS), 0) < iota((SLOTS, SLOTS), 1))
    rank = jnp.sum(to * nn(to.astype(BF16), before), axis=0, keepdims=True)
    place = onehot(
        rank.astype(I32) + 32 * lane0 == iota((W, SLOTS), 0)
    )
    sample1 = ((iota((1, SLOTS), 1) & (SAMP - 1)) + 1).astype(F32)
    packed = jnp.concatenate([to * flat[1], to * flat[2], to * sample1], axis=0).astype(BF16)
    placed = nt(packed, place)
    colpart = 32.0 * placed[0:NS] + placed[32 : 32 + NS]
    samppart = pltpu.roll(placed[64 : 64 + NS], 32, 1)
    dests = jnp.zeros((1, W), I32)
    lane = iota((1, W), 1)
    dlane = 32 * lax.rem(mine + 2, 4)
    for j in range(NB):
        dests = jnp.where(lane == dlane + j, dest_s[j], dests)
    msg[:, 0, :] = colpart + samppart + dests.astype(F32)

    loads[0].wait()
    hi, lo = split2(tbl[...])
    hl[hotc:cols, 0:W] = hi
    hl[hotc:cols, W : 2 * W] = lo
    offs = jnp.zeros((HOTD, ROWS), I32)
    hrow = iota((HOTD, ROWS), 0)
    for k in range(HOTD):
        offs = jnp.where(hrow == k, off_s[k], offs)
    picked = nn(onehot(offs == iota((HOTD, ROWS), 1)), hl[hotc:cols, :])
    hotloc[...] = picked[:, :W] + picked[:, W:]
    for r in range(BLK):
        abuf[r] = tbl[pl.ds(r, NB, stride=BLK), :]

    def tell(sem):
        pl.semaphore_signal(sem, inc=1, device_id={"shard": sib}, device_id_type=MESH)

    @pl.when(core == 0)
    def _():
        pl.semaphore_wait(barrier, NS - 1)
        tell(column_sem)

    @pl.when(core == 1)
    def _():
        pl.semaphore_wait(column_sem, 1)

    pltpu.make_async_copy(msg.at[pl.ds(me, 1)], req.at[pl.ds(mine, 1)], req_recv).start()

    far_first(me, NS, lambda peer: pltpu.make_async_remote_copy(
        src_ref=msg.at[pl.ds(peer, 1)], dst_ref=req.at[pl.ds(mine, 1)],
        send_sem=req_send, recv_sem=req_recv,
        device_id={"shard": peer}, device_id_type=MESH,
    ).start())

    def push(src, dst, send_sem, recv_sem, peer):
        pltpu.make_async_remote_copy(
            src_ref=src, dst_ref=dst, send_sem=send_sem, recv_sem=recv_sem,
            device_id={"shard": peer}, device_id_type=MESH,
        ).start()

    def relay(peer, start, count):
        src = abuf.at[pl.ds(first_row(peer) + start, count)]
        dst = xbuf.at[
            start : start + count, pl.ds(pl.multiple_of(me * NB, NB), NB), :
        ]
        return src, dst

    def by_count(peer, act):
        @pl.when(lax.rem(peer, 3) < 2)
        def _():
            act(3)

        @pl.when(lax.rem(peer, 3) == 2)
        def _():
            act(2)

    pltpu.make_async_copy(*relay(me, 0, 1), one_recv.at[0]).start()
    pltpu.make_async_copy(*relay(me, 1, 1), one_recv.at[1]).start()

    @pl.when(three)
    def _():
        pltpu.make_async_copy(*relay(me, 2, 1), one_recv.at[2]).start()

    far_first(
        me, NS, lambda peer: push(*relay(peer, 0, 1), one_send, one_recv.at[0], peer)
    )
    far_first(
        me, NS, lambda peer: push(*relay(peer, 1, 1), one_send, one_recv.at[1], peer)
    )

    def third(peer):
        @pl.when(lax.rem(peer, 3) < 2)
        def _():
            push(*relay(peer, 2, 1), one_send, one_recv.at[2], peer)

    far_first(me, NS, third)

    @pl.when(core == 1)
    def _():
        pl.semaphore_wait(barrier, 2 * ng - 1)
        tell(plane_sem)

    @pl.when(core == 0)
    def _():
        pl.semaphore_wait(plane_sem, 1)

    hot_here = hotbuf.at[pl.ds(pl.multiple_of(grp * HOTD, HOTD), HOTD)]
    pltpu.make_async_copy(hotloc, hot_here, hot_recv).start()

    far_first(grp, ng, lambda peer: pltpu.make_async_remote_copy(
        src_ref=hotloc, dst_ref=hot_here, send_sem=hot_send, recv_sem=hot_recv,
        device_id={"grp": peer}, device_id_type=MESH,
    ).start())

    wait_bytes(req, req_recv)
    asked = req[:, 0, :]
    b = iota((W, NBLK), 1)
    bs = (((b >> 3) & 1) * NZ) + (b >> 4)
    dlanes = onehot(iota((W, NBLK), 0) == 32 * ((bs + 2) & 3) + (b & 7))
    bs24 = bs[0:NS]
    target = jnp.sum(
        jnp.where(iota((NS, NBLK), 0) == bs24, nn(asked.astype(BF16), dlanes), 0.0),
        axis=0, keepdims=True,
    ).astype(I32)
    goes = jnp.where(iota((32, NBLK), 0) == target, 1.0, 0.0)
    earlier = onehot(iota((NBLK, NBLK), 0) < iota((NBLK, NBLK), 1))
    seat = nn(goes.astype(BF16), earlier) + (NB * iota((32, NBLK), 0)).astype(F32)
    seat = jnp.sum(goes * seat, axis=0, keepdims=True).astype(I32)
    perm = onehot(iota((NBLK, NBLK), 0) == seat)

    def reorder(i):
        x = xbuf[i]
        hi = x.astype(BF16)
        rest = x - hi.astype(F32)
        mid = rest.astype(BF16)
        low = (rest - mid.astype(F32)).astype(BF16)
        y = nn(perm, jnp.concatenate([hi, mid, low], axis=1))
        ybuf[i] = (y[:, :W] + y[:, W : 2 * W]) + y[:, 2 * W :]

    def deliver(peer, start, count):
        src = ybuf.at[
            start : start + count, pl.ds(pl.multiple_of(peer * NB, NB), NB), :
        ]
        return src, moved.at[pl.ds(first_row(me) + start, count)]

    def deliver_all(start, count):
        pltpu.make_async_copy(*deliver(me, start, count), two_recv).start()
        far_first(
            me, NS,
            lambda peer: push(*deliver(peer, start, count), two_send, two_recv, peer),
        )

    who = iota((NS, W), 0)
    spot = (iota((NS, W), 1) >> 5) & 3
    first = jnp.where(spot == (who & 3), asked, 0.0)
    second = pltpu.roll(jnp.where(spot == ((who + 1) & 3), asked, 0.0), W - 32, 1)
    pad = jnp.zeros((8 - GROUPS, W), F32)
    gather4 = lambda x: jnp.concatenate(
        [jnp.sum(x[4 * g : 4 * g + 4], axis=0, keepdims=True) for g in range(GROUPS)] + [pad],
        axis=0,
    )
    colv[...] = gather4(first).astype(I32)
    samp = gather4(second).astype(I32)
    keyv[...] = jnp.where(samp > 0, samp - 1 + ((iota((8, W), 1) >> 5) << 5), -1)

    @pl.loop(0, GROUPS)
    def _(g):
        key = keyv[pl.ds(g, 1), :]
        want = colv[pl.ds(g, 1), :]
        sums = onehot(iota((W, W), 0) == key)
        names = onehot(iota((cols, W), 0) == want)
        cmat[pl.ds(pl.multiple_of(g * W, W), W), :] = nt(sums, names).astype(BF16)

    wait_bytes(xbuf.at[0:1], one_recv.at[0])
    reorder(0)
    deliver_all(0, 1)

    wait_bytes(xbuf.at[1:2], one_recv.at[1])
    reorder(1)
    deliver_all(1, 1)

    wait_bytes(hotbuf, hot_recv)
    hi, lo = split2(hotbuf[...])
    hl[0:hotc, 0:W] = hi
    hl[0:hotc, W : 2 * W] = lo
    half = NZ * SAMP
    for h in range(2):
        part = nn(cmat[half * h : half * (h + 1), :], hl[...])
        pbuf[h] = (part[:, :W] + part[:, W:]).reshape(NZ, SAMP, W)
    to_sib = pltpu.make_async_remote_copy(
        src_ref=pbuf.at[1 - core], dst_ref=sbuf, send_sem=sib_send, recv_sem=sib_recv,
        device_id={"shard": sib}, device_id_type=MESH,
    )
    to_sib.start()
    to_sib.wait_recv()
    pbuf[core] += sbuf[...]
    pltpu.make_async_copy(pbuf.at[core, chip], pin.at[HOP], sum_recv).start()

    def chip_at(step):
        return lax.rem(chip + step + NZ, NZ)

    def send_sum(step, via, dst, recv_sem):
        push(
            pbuf.at[core, chip_at(step)], dst, sum_send, recv_sem,
            2 * chip_at(via) + core,
        )

    send_sum(6, 3 + 6 * core, rin.at[4], far_recv)
    for i, step in enumerate((-5, 5, -4, 4)):
        send_sum(step, step - HOP if step > 0 else step + HOP, rin.at[i], far_recv)
    for step in (-2, 2, -1, 1):
        send_sum(step, step, pin.at[HOP + step], sum_recv)


    @pl.when(three)
    def _():
        wait_bytes(xbuf.at[2:3], one_recv.at[2])
        reorder(2)
        deliver_all(2, 1)

    wait_bytes(rin, far_recv)
    pbuf[core, chip_at(-HOP)] += rin[0] + rin[2]
    pbuf[core, chip_at(HOP)] += rin[1] + rin[3]
    pbuf[core, chip_at(HOP + 6 * core)] += rin[4]
    for step in (-HOP, HOP):
        send_sum(step, step, pin.at[HOP + step], sum_recv)
    wait_bytes(pin, sum_recv)
    total = pin[0]
    for z in range(1, 2 * HOP + 1):
        total += pin[z]
    pooled[...] = total / lens.astype(F32)

    wait_bytes(moved, two_recv)
    to_sib.wait_send()
    wait_bytes(req.at[0 : NS - 1], req_send)
    wait_bytes(hotbuf.at[0 : hotc - HOTD], hot_send)
    wait_bytes(pbuf.at[0, 0 : NZ - 1], sum_send)

    by_count(me, lambda n: wait_bytes(abuf.at[0 : BLK - n], one_send))
    by_count(me, lambda n: wait_bytes(xbuf.at[0:n, 0 : NBLK - NB, :], two_send))


def finish(moved, sums, table, pooled):
    for r in range(BLK):
        table[pl.ds(r, NB, stride=BLK), :] = moved[r]
    pooled[...] = sums[...]


def local(table, hot_offsets, cold_dest, bag_ids, bag_len):
    ng = lax.axis_size("grp")
    hotc = ng * HOTD
    cols = hotc + ROWS
    dma = pltpu.SemaphoreType.DMA
    moved, pooled = pl.pallas_call(
        functools.partial(kernel, ng),
        out_shape=(
            jax.ShapeDtypeStruct((BLK, NB, W), F32),
            jax.ShapeDtypeStruct((SAMP, W), F32),
        ),
        in_specs=[pl.BlockSpec(memory_space=pltpu.HBM)] * 5,
        out_specs=(
            pl.BlockSpec(memory_space=pl.ANY),
            pl.BlockSpec(memory_space=pltpu.VMEM),
        ),
        scratch_shapes=[
            pltpu.VMEM((ROWS, W), F32),
            pltpu.VMEM((BAG, SAMP), I32),
            pltpu.SMEM((HOTD,), I32),
            pltpu.SMEM((NB,), I32),
            pltpu.SMEM((SAMP,), I32),
            pltpu.VMEM((BLK, NB, W), F32),
            pltpu.VMEM((cols, 2 * W), BF16),
            pltpu.VMEM((HOTD, W), F32),
            pltpu.VMEM((hotc, W), F32),
            pltpu.VMEM((NS, 1, W), F32),
            pltpu.VMEM((NS, 1, W), F32),
            pltpu.VMEM((3, NBLK, W), F32),
            pltpu.VMEM((3, NBLK, W), F32),
            pltpu.VMEM((NS * SAMP, cols), BF16),
            pltpu.VMEM((2, NZ, SAMP, W), F32),
            pltpu.VMEM((NZ, SAMP, W), F32),
            pltpu.VMEM((5, SAMP, W), F32),
            pltpu.VMEM((2 * HOP + 1, SAMP, W), F32),
            pltpu.VMEM((8, W), I32),
            pltpu.VMEM((8, W), I32),
            dma((5,)),
        ]
        + [dma(())] * 5
        + [dma((3,))]
        + [dma(())] * 7
        + [pltpu.SemaphoreType.REGULAR] * 2,
        compiler_params=pltpu.CompilerParams(
            collective_id=0, has_side_effects=True, vmem_limit_bytes=24 * 1024 * 1024
        ),
    )(
        *(
            pltpu.with_memory_space_constraint(x, pltpu.HBM)
            for x in (table, hot_offsets, cold_dest, bag_ids.T, bag_len)
        )
    )
    return pl.pallas_call(
        finish,
        out_shape=(
            jax.ShapeDtypeStruct((ROWS, W), F32),
            jax.ShapeDtypeStruct((SAMP, W), F32),
        ),
        in_specs=[pl.BlockSpec(memory_space=pltpu.VMEM)] * 2,
        out_specs=[pl.BlockSpec(memory_space=pltpu.VMEM)] * 2,
    )(
        pltpu.with_memory_space_constraint(moved, pltpu.VMEM),
        pltpu.with_memory_space_constraint(pooled, pltpu.VMEM),
    )


def solution(mesh):
    return jax.shard_map(
        local,
        mesh=mesh,
        in_specs=(
            P(("grp", "shard"), None),
            P(("grp", "shard")),
            P(("grp", "shard")),
            P(("grp", "shard"), None),
            P(("grp", "shard")),
        ),
        out_specs=(P(("grp", "shard"), None), P(("grp", "shard"), None)),
        check_vma=False,
    )
```

```python
import functools

import jax
import jax.numpy as jnp
from jax import lax
from jax.experimental import pallas as pl
from jax.experimental.pallas import tpu as pltpu
from jax.sharding import PartitionSpec as P

MESH = pl.DeviceIdType.MESH
F32 = jnp.float32
BF16 = jnp.bfloat16
I32 = jnp.int32

NS = 24
NZ = 12
HOP = 3
NB = 8
BLK = 64
W = 128
NBLK = NS * NB
SAMP = 32
BAG = 16
SLOTS = SAMP * BAG
HOTD = 16
ROWS = NB * BLK
GROUPS = NS // 4


def iota(shape, axis):
    return lax.broadcasted_iota(I32, shape, axis)


def onehot(mask):
    return jnp.where(mask, 1.0, 0.0).astype(BF16)


def nt(a, b):
    return lax.dot_general(a, b, (((1,), (1,)), ((), ())), preferred_element_type=F32)


def nn(a, b):
    return jnp.dot(a, b, preferred_element_type=F32)


def split2(x):
    hi = x.astype(BF16)
    return hi, (x - hi.astype(F32)).astype(BF16)


def first_row(m):
    return 8 * (m // 3) + 3 * lax.rem(m, 3)


def order(s):
    return lax.rem(s, 2) * NZ + s // 2


def far_first(me, n, act):
    act(lax.rem(me + n // 2, n))

    @pl.loop(1, n // 2)
    def _(q):
        act(lax.rem(me + n // 2 - q, n))
        act(lax.rem(me + n // 2 + q, n))


def far_first_plane(me, n, act):
    nx, ny = (4, 8) if n == 32 else (1, n)
    x, y = me // ny, lax.rem(me, ny)
    steps = [(i, j) for i in range(nx) for j in range(ny) if i or j]
    steps.sort(key=lambda p: min(p[0], nx - p[0]) + min(p[1], ny - p[1]), reverse=True)
    for i, j in steps:
        act(lax.rem(x + i, nx) * ny + lax.rem(y + j, ny))


def wait_bytes(ref, sem):
    pltpu.make_async_copy(ref, ref, sem).wait()


def kernel(
    ng,
    table_h, off_h, dest_h, ids_h, len_h,
    moved, pooled,
    tbl, ids, off_s, dest_s, len_s,
    abuf, hl, hotloc, hotbuf, msg, req, xbuf, ybuf, cmat, pbuf, sbuf, rin, pin, colv, keyv,
    load_sem, req_send, req_recv, hot_send, hot_recv, one_send, one_recv, two_send, two_recv,
    sib_send, sib_recv, sum_send, sum_recv, far_recv,
    column_sem, plane_sem,
):
    hotc = ng * HOTD
    cols = hotc + ROWS
    me = lax.axis_index("shard")
    grp = lax.axis_index("grp")
    core = lax.rem(me, 2)
    chip = me // 2
    sib = me + 1 - 2 * core
    mine = order(me)
    lane0 = lax.rem(mine, 4)
    three = lax.rem(me, 3) < 2

    barrier = pltpu.get_barrier_semaphore()

    def greet(where):
        pl.semaphore_signal(barrier, inc=1, device_id=where, device_id_type=MESH)

    far_first(chip, NZ, lambda z: greet({"shard": 2 * z}))
    far_first_plane(grp, ng, lambda g: greet({"grp": g, "shard": 2 * chip + 1}))
    greet({"shard": sib})

    loads = [
        pltpu.make_async_copy(table_h, tbl, load_sem.at[0]),
        pltpu.make_async_copy(ids_h, ids, load_sem.at[1]),
        pltpu.make_async_copy(len_h, len_s, load_sem.at[2]),
        pltpu.make_async_copy(off_h, off_s, load_sem.at[3]),
        pltpu.make_async_copy(dest_h, dest_s, load_sem.at[4]),
    ]
    for load in loads:
        load.start()

    for load in loads[1:]:
        load.wait()

    lens = jnp.zeros((SAMP, W), I32)
    row = iota((SAMP, W), 0)
    for n in range(SAMP):
        lens = jnp.where(row == n, len_s[n], lens)
    bag = ids[...]
    hot_total = hotc * NS
    is_hot = bag < hot_total
    owner = bag >> 4
    turn = (owner * 43691) >> 20
    cold = jnp.maximum(bag - hot_total, 0)
    shard = jnp.where(is_hot, owner - turn * NS, cold >> 9)
    col = jnp.where(is_hot, turn * HOTD + (bag & (HOTD - 1)), hotc + (cold & (ROWS - 1)))
    square = iota((SAMP, SAMP), 0) == iota((SAMP, SAMP), 1)
    lens_row = jnp.sum(jnp.where(square, lens[:, :SAMP], 0), axis=0, keepdims=True)
    live = iota((BAG, SAMP), 0) < lens_row
    shard = jnp.where(live, shard, 31)
    fields = jnp.concatenate([shard, col >> 5, col & 31], axis=0).astype(F32).astype(BF16)
    spread = nn(fields, onehot(iota((SAMP, SLOTS), 0) == (iota((SAMP, SLOTS), 1) & (SAMP - 1))))
    own = iota((BAG, SLOTS), 0) == (iota((BAG, SLOTS), 1) >> 5)
    flat = [
        jnp.sum(jnp.where(own, spread[BAG * i : BAG * (i + 1)], 0.0), axis=0, keepdims=True)
        for i in range(3)
    ]
    to = jnp.where(flat[0] == iota((32, SLOTS), 0).astype(F32), 1.0, 0.0)
    to = jnp.where(iota((32, SLOTS), 0) < NS, to, 0.0)
    before = onehot(iota((SLOTS, SLOTS), 0) < iota((SLOTS, SLOTS), 1))
    rank = jnp.sum(to * nn(to.astype(BF16), before), axis=0, keepdims=True)
    place = onehot(
        rank.astype(I32) + 32 * lane0 == iota((W, SLOTS), 0)
    )
    sample1 = ((iota((1, SLOTS), 1) & (SAMP - 1)) + 1).astype(F32)
    packed = jnp.concatenate([to * flat[1], to * flat[2], to * sample1], axis=0).astype(BF16)
    placed = nt(packed, place)
    colpart = 32.0 * placed[0:NS] + placed[32 : 32 + NS]
    samppart = pltpu.roll(placed[64 : 64 + NS], 32, 1)
    dests = jnp.zeros((1, W), I32)
    lane = iota((1, W), 1)
    dlane = 32 * lax.rem(mine + 2, 4)
    for j in range(NB):
        dests = jnp.where(lane == dlane + j, dest_s[j], dests)
    msg[:, 0, :] = colpart + samppart + dests.astype(F32)

    loads[0].wait()
    hi, lo = split2(tbl[...])
    hl[hotc:cols, 0:W] = hi
    hl[hotc:cols, W : 2 * W] = lo
    offs = jnp.zeros((HOTD, ROWS), I32)
    hrow = iota((HOTD, ROWS), 0)
    for k in range(HOTD):
        offs = jnp.where(hrow == k, off_s[k], offs)
    picked = nn(onehot(offs == iota((HOTD, ROWS), 1)), hl[hotc:cols, :])
    hotloc[...] = picked[:, :W] + picked[:, W:]
    for r in range(BLK):
        abuf[r] = tbl[pl.ds(r, NB, stride=BLK), :]

    def tell(sem):
        pl.semaphore_signal(sem, inc=1, device_id={"shard": sib}, device_id_type=MESH)

    @pl.when(core == 0)
    def _():
        pl.semaphore_wait(barrier, NS - 1)
        tell(column_sem)

    @pl.when(core == 1)
    def _():
        pl.semaphore_wait(column_sem, 1)

    pltpu.make_async_copy(msg.at[pl.ds(me, 1)], req.at[pl.ds(mine, 1)], req_recv).start()

    far_first(me, NS, lambda peer: pltpu.make_async_remote_copy(
        src_ref=msg.at[pl.ds(peer, 1)], dst_ref=req.at[pl.ds(mine, 1)],
        send_sem=req_send, recv_sem=req_recv,
        device_id={"shard": peer}, device_id_type=MESH,
    ).start())

    def push(src, dst, send_sem, recv_sem, peer):
        pltpu.make_async_remote_copy(
            src_ref=src, dst_ref=dst, send_sem=send_sem, recv_sem=recv_sem,
            device_id={"shard": peer}, device_id_type=MESH,
        ).start()

    def relay(peer, start, count):
        src = abuf.at[pl.ds(first_row(peer) + start, count)]
        dst = xbuf.at[
            start : start + count, pl.ds(pl.multiple_of(me * NB, NB), NB), :
        ]
        return src, dst

    def by_count(peer, act):
        @pl.when(lax.rem(peer, 3) < 2)
        def _():
            act(3)

        @pl.when(lax.rem(peer, 3) == 2)
        def _():
            act(2)

    pltpu.make_async_copy(*relay(me, 0, 1), one_recv.at[0]).start()
    pltpu.make_async_copy(*relay(me, 1, 1), one_recv.at[1]).start()

    @pl.when(three)
    def _():
        pltpu.make_async_copy(*relay(me, 2, 1), one_recv.at[2]).start()

    far_first(
        me, NS, lambda peer: push(*relay(peer, 0, 1), one_send, one_recv.at[0], peer)
    )
    far_first(
        me, NS, lambda peer: push(*relay(peer, 1, 1), one_send, one_recv.at[1], peer)
    )

    def third(peer):
        @pl.when(lax.rem(peer, 3) < 2)
        def _():
            push(*relay(peer, 2, 1), one_send, one_recv.at[2], peer)

    far_first(me, NS, third)

    @pl.when(core == 1)
    def _():
        pl.semaphore_wait(barrier, 2 * ng - 1)
        tell(plane_sem)

    @pl.when(core == 0)
    def _():
        pl.semaphore_wait(plane_sem, 1)

    hot_here = hotbuf.at[pl.ds(pl.multiple_of(grp * HOTD, HOTD), HOTD)]
    pltpu.make_async_copy(hotloc, hot_here, hot_recv).start()

    far_first_plane(grp, ng, lambda peer: pltpu.make_async_remote_copy(
        src_ref=hotloc, dst_ref=hot_here, send_sem=hot_send, recv_sem=hot_recv,
        device_id={"grp": peer}, device_id_type=MESH,
    ).start())

    wait_bytes(req, req_recv)
    asked = req[:, 0, :]
    b = iota((W, NBLK), 1)
    bs = (((b >> 3) & 1) * NZ) + (b >> 4)
    dlanes = onehot(iota((W, NBLK), 0) == 32 * ((bs + 2) & 3) + (b & 7))
    bs24 = bs[0:NS]
    target = jnp.sum(
        jnp.where(iota((NS, NBLK), 0) == bs24, nn(asked.astype(BF16), dlanes), 0.0),
        axis=0, keepdims=True,
    ).astype(I32)
    goes = jnp.where(iota((32, NBLK), 0) == target, 1.0, 0.0)
    earlier = onehot(iota((NBLK, NBLK), 0) < iota((NBLK, NBLK), 1))
    seat = nn(goes.astype(BF16), earlier) + (NB * iota((32, NBLK), 0)).astype(F32)
    seat = jnp.sum(goes * seat, axis=0, keepdims=True).astype(I32)
    perm = onehot(iota((NBLK, NBLK), 0) == seat)

    def reorder(i):
        x = xbuf[i]
        hi = x.astype(BF16)
        rest = x - hi.astype(F32)
        mid = rest.astype(BF16)
        low = (rest - mid.astype(F32)).astype(BF16)
        y = nn(perm, jnp.concatenate([hi, mid, low], axis=1))
        ybuf[i] = (y[:, :W] + y[:, W : 2 * W]) + y[:, 2 * W :]

    def deliver(peer, start, count):
        src = ybuf.at[
            start : start + count, pl.ds(pl.multiple_of(peer * NB, NB), NB), :
        ]
        return src, moved.at[pl.ds(first_row(me) + start, count)]

    def deliver_all(start, count):
        pltpu.make_async_copy(*deliver(me, start, count), two_recv).start()
        far_first(
            me, NS,
            lambda peer: push(*deliver(peer, start, count), two_send, two_recv, peer),
        )

    who = iota((NS, W), 0)
    spot = (iota((NS, W), 1) >> 5) & 3
    first = jnp.where(spot == (who & 3), asked, 0.0)
    second = pltpu.roll(jnp.where(spot == ((who + 1) & 3), asked, 0.0), W - 32, 1)
    pad = jnp.zeros((8 - GROUPS, W), F32)
    gather4 = lambda x: jnp.concatenate(
        [jnp.sum(x[4 * g : 4 * g + 4], axis=0, keepdims=True) for g in range(GROUPS)] + [pad],
        axis=0,
    )
    colv[...] = gather4(first).astype(I32)
    samp = gather4(second).astype(I32)
    keyv[...] = jnp.where(samp > 0, samp - 1 + ((iota((8, W), 1) >> 5) << 5), -1)

    @pl.loop(0, GROUPS)
    def _(g):
        key = keyv[pl.ds(g, 1), :]
        want = colv[pl.ds(g, 1), :]
        sums = onehot(iota((W, W), 0) == key)
        names = onehot(iota((cols, W), 0) == want)
        cmat[pl.ds(pl.multiple_of(g * W, W), W), :] = nt(sums, names).astype(BF16)

    wait_bytes(xbuf.at[0:1], one_recv.at[0])
    reorder(0)
    deliver_all(0, 1)

    wait_bytes(xbuf.at[1:2], one_recv.at[1])
    reorder(1)
    deliver_all(1, 1)

    wait_bytes(hotbuf, hot_recv)
    hi, lo = split2(hotbuf[...])
    hl[0:hotc, 0:W] = hi
    hl[0:hotc, W : 2 * W] = lo
    half = NZ * SAMP
    for h in range(2):
        part = nn(cmat[half * h : half * (h + 1), :], hl[...])
        pbuf[h] = (part[:, :W] + part[:, W:]).reshape(NZ, SAMP, W)
    to_sib = pltpu.make_async_remote_copy(
        src_ref=pbuf.at[1 - core], dst_ref=sbuf, send_sem=sib_send, recv_sem=sib_recv,
        device_id={"shard": sib}, device_id_type=MESH,
    )
    to_sib.start()
    to_sib.wait_recv()
    pbuf[core] += sbuf[...]
    pltpu.make_async_copy(pbuf.at[core, chip], pin.at[HOP], sum_recv).start()

    def chip_at(step):
        return lax.rem(chip + step + NZ, NZ)

    def send_sum(step, via, dst, recv_sem):
        push(
            pbuf.at[core, chip_at(step)], dst, sum_send, recv_sem,
            2 * chip_at(via) + core,
        )

    send_sum(6, 3 + 6 * core, rin.at[4], far_recv)
    for i, step in enumerate((-5, 5, -4, 4)):
        send_sum(step, step - HOP if step > 0 else step + HOP, rin.at[i], far_recv)
    for step in (-2, 2, -1, 1):
        send_sum(step, step, pin.at[HOP + step], sum_recv)


    @pl.when(three)
    def _():
        wait_bytes(xbuf.at[2:3], one_recv.at[2])
        reorder(2)
        deliver_all(2, 1)

    wait_bytes(rin, far_recv)
    pbuf[core, chip_at(-HOP)] += rin[0] + rin[2]
    pbuf[core, chip_at(HOP)] += rin[1] + rin[3]
    pbuf[core, chip_at(HOP + 6 * core)] += rin[4]
    for step in (-HOP, HOP):
        send_sum(step, step, pin.at[HOP + step], sum_recv)
    wait_bytes(pin, sum_recv)
    total = pin[0]
    for z in range(1, 2 * HOP + 1):
        total += pin[z]
    pooled[...] = total / lens.astype(F32)

    wait_bytes(moved, two_recv)
    to_sib.wait_send()
    wait_bytes(req.at[0 : NS - 1], req_send)
    wait_bytes(hotbuf.at[0 : hotc - HOTD], hot_send)
    wait_bytes(pbuf.at[0, 0 : NZ - 1], sum_send)

    by_count(me, lambda n: wait_bytes(abuf.at[0 : BLK - n], one_send))
    by_count(me, lambda n: wait_bytes(xbuf.at[0:n, 0 : NBLK - NB, :], two_send))


def finish(moved, sums, table, pooled):
    for r in range(BLK):
        table[pl.ds(r, NB, stride=BLK), :] = moved[r]
    pooled[...] = sums[...]


def local(table, hot_offsets, cold_dest, bag_ids, bag_len):
    ng = lax.axis_size("grp")
    hotc = ng * HOTD
    cols = hotc + ROWS
    dma = pltpu.SemaphoreType.DMA
    moved, pooled = pl.pallas_call(
        functools.partial(kernel, ng),
        out_shape=(
            jax.ShapeDtypeStruct((BLK, NB, W), F32),
            jax.ShapeDtypeStruct((SAMP, W), F32),
        ),
        in_specs=[pl.BlockSpec(memory_space=pltpu.HBM)] * 5,
        out_specs=(
            pl.BlockSpec(memory_space=pl.ANY),
            pl.BlockSpec(memory_space=pltpu.VMEM),
        ),
        scratch_shapes=[
            pltpu.VMEM((ROWS, W), F32),
            pltpu.VMEM((BAG, SAMP), I32),
            pltpu.SMEM((HOTD,), I32),
            pltpu.SMEM((NB,), I32),
            pltpu.SMEM((SAMP,), I32),
            pltpu.VMEM((BLK, NB, W), F32),
            pltpu.VMEM((cols, 2 * W), BF16),
            pltpu.VMEM((HOTD, W), F32),
            pltpu.VMEM((hotc, W), F32),
            pltpu.VMEM((NS, 1, W), F32),
            pltpu.VMEM((NS, 1, W), F32),
            pltpu.VMEM((3, NBLK, W), F32),
            pltpu.VMEM((3, NBLK, W), F32),
            pltpu.VMEM((NS * SAMP, cols), BF16),
            pltpu.VMEM((2, NZ, SAMP, W), F32),
            pltpu.VMEM((NZ, SAMP, W), F32),
            pltpu.VMEM((5, SAMP, W), F32),
            pltpu.VMEM((2 * HOP + 1, SAMP, W), F32),
            pltpu.VMEM((8, W), I32),
            pltpu.VMEM((8, W), I32),
            dma((5,)),
        ]
        + [dma(())] * 5
        + [dma((3,))]
        + [dma(())] * 7
        + [pltpu.SemaphoreType.REGULAR] * 2,
        compiler_params=pltpu.CompilerParams(
            collective_id=0, has_side_effects=True, vmem_limit_bytes=24 * 1024 * 1024
        ),
    )(
        *(
            pltpu.with_memory_space_constraint(x, pltpu.HBM)
            for x in (table, hot_offsets, cold_dest, bag_ids.T, bag_len)
        )
    )
    return pl.pallas_call(
        finish,
        out_shape=(
            jax.ShapeDtypeStruct((ROWS, W), F32),
            jax.ShapeDtypeStruct((SAMP, W), F32),
        ),
        in_specs=[pl.BlockSpec(memory_space=pltpu.VMEM)] * 2,
        out_specs=[pl.BlockSpec(memory_space=pltpu.VMEM)] * 2,
    )(
        pltpu.with_memory_space_constraint(moved, pltpu.VMEM),
        pltpu.with_memory_space_constraint(pooled, pltpu.VMEM),
    )


def solution(mesh):
    return jax.shard_map(
        local,
        mesh=mesh,
        in_specs=(
            P(("grp", "shard"), None),
            P(("grp", "shard")),
            P(("grp", "shard")),
            P(("grp", "shard"), None),
            P(("grp", "shard")),
        ),
        out_specs=(P(("grp", "shard"), None), P(("grp", "shard"), None)),
        check_vma=False,
    )
```

```python
import functools

import jax
import jax.numpy as jnp
from jax import lax
from jax.experimental import pallas as pl
from jax.experimental.pallas import tpu as pltpu
from jax.sharding import PartitionSpec as P

MESH = pl.DeviceIdType.MESH
F32 = jnp.float32
BF16 = jnp.bfloat16
I32 = jnp.int32

NS = 24
NZ = 12
HOP = 3
NB = 8
BLK = 64
W = 128
NBLK = NS * NB
SAMP = 32
BAG = 16
SLOTS = SAMP * BAG
HOTD = 16
ROWS = NB * BLK
GROUPS = NS // 4


def iota(shape, axis):
    return lax.broadcasted_iota(I32, shape, axis)


def onehot(mask):
    return jnp.where(mask, 1.0, 0.0).astype(BF16)


def nt(a, b):
    return lax.dot_general(a, b, (((1,), (1,)), ((), ())), preferred_element_type=F32)


def nn(a, b):
    return jnp.dot(a, b, preferred_element_type=F32)


def split2(x):
    hi = x.astype(BF16)
    return hi, (x - hi.astype(F32)).astype(BF16)


def first_row(m):
    return 8 * (m // 3) + 3 * lax.rem(m, 3)


def order(s):
    return lax.rem(s, 2) * NZ + s // 2


def far_first(me, n, act):
    act(lax.rem(me + n // 2, n))

    @pl.loop(1, n // 2)
    def _(q):
        act(lax.rem(me + n // 2 - q, n))
        act(lax.rem(me + n // 2 + q, n))


def far_first_plane(me, n, act):
    nx, ny = (4, 8) if n == 32 else (1, n)
    x, y = me // ny, lax.rem(me, ny)
    steps = [(i, j) for i in range(nx) for j in range(ny) if i or j]
    steps.sort(key=lambda p: min(p[0], nx - p[0]) + min(p[1], ny - p[1]), reverse=True)
    for i, j in steps:
        act(lax.rem(x + i, nx) * ny + lax.rem(y + j, ny))


def wait_bytes(ref, sem):
    pltpu.make_async_copy(ref, ref, sem).wait()


def kernel(
    ng,
    table_h, off_h, dest_h, ids_h, len_h,
    moved, pooled,
    tbl, ids, off_s, dest_s, len_s,
    abuf, hl, hotloc, hotbuf, msg, req, xbuf, ybuf, cmat, pbuf, sbuf, rin, pin, colv, keyv,
    load_sem, req_send, req_recv, hot_send, hot_recv, one_send, one_recv, two_send, two_recv,
    sib_send, sib_recv, sum_send, sum_recv, far_recv,
    column_sem, plane_sem,
):
    hotc = ng * HOTD
    cols = hotc + ROWS
    me = lax.axis_index("shard")
    grp = lax.axis_index("grp")
    core = lax.rem(me, 2)
    chip = me // 2
    sib = me + 1 - 2 * core
    mine = order(me)
    lane0 = lax.rem(mine, 4)
    three = lax.rem(me, 3) < 2

    barrier = pltpu.get_barrier_semaphore()

    def greet(where):
        pl.semaphore_signal(barrier, inc=1, device_id=where, device_id_type=MESH)

    far_first(chip, NZ, lambda z: greet({"shard": 2 * z}))
    far_first_plane(grp, ng, lambda g: greet({"grp": g, "shard": 2 * chip + 1}))
    greet({"shard": sib})

    loads = [
        pltpu.make_async_copy(table_h, tbl, load_sem.at[0]),
        pltpu.make_async_copy(ids_h, ids, load_sem.at[1]),
        pltpu.make_async_copy(len_h, len_s, load_sem.at[2]),
        pltpu.make_async_copy(off_h, off_s, load_sem.at[3]),
        pltpu.make_async_copy(dest_h, dest_s, load_sem.at[4]),
    ]
    for load in loads:
        load.start()

    for load in loads[1:]:
        load.wait()

    lens = jnp.zeros((SAMP, W), I32)
    row = iota((SAMP, W), 0)
    for n in range(SAMP):
        lens = jnp.where(row == n, len_s[n], lens)
    bag = ids[...]
    hot_total = hotc * NS
    is_hot = bag < hot_total
    owner = bag >> 4
    turn = (owner * 43691) >> 20
    cold = jnp.maximum(bag - hot_total, 0)
    shard = jnp.where(is_hot, owner - turn * NS, cold >> 9)
    col = jnp.where(is_hot, turn * HOTD + (bag & (HOTD - 1)), hotc + (cold & (ROWS - 1)))
    square = iota((SAMP, SAMP), 0) == iota((SAMP, SAMP), 1)
    lens_row = jnp.sum(jnp.where(square, lens[:, :SAMP], 0), axis=0, keepdims=True)
    live = iota((BAG, SAMP), 0) < lens_row
    shard = jnp.where(live, shard, 31)
    fields = jnp.concatenate([shard, col >> 5, col & 31], axis=0).astype(F32).astype(BF16)
    spread = nn(fields, onehot(iota((SAMP, SLOTS), 0) == (iota((SAMP, SLOTS), 1) & (SAMP - 1))))
    own = iota((BAG, SLOTS), 0) == (iota((BAG, SLOTS), 1) >> 5)
    flat = [
        jnp.sum(jnp.where(own, spread[BAG * i : BAG * (i + 1)], 0.0), axis=0, keepdims=True)
        for i in range(3)
    ]
    to = jnp.where(flat[0] == iota((32, SLOTS), 0).astype(F32), 1.0, 0.0)
    to = jnp.where(iota((32, SLOTS), 0) < NS, to, 0.0)
    before = onehot(iota((SLOTS, SLOTS), 0) < iota((SLOTS, SLOTS), 1))
    rank = jnp.sum(to * nn(to.astype(BF16), before), axis=0, keepdims=True)
    place = onehot(
        rank.astype(I32) + 32 * lane0 == iota((W, SLOTS), 0)
    )
    sample1 = ((iota((1, SLOTS), 1) & (SAMP - 1)) + 1).astype(F32)
    packed = jnp.concatenate([to * flat[1], to * flat[2], to * sample1], axis=0).astype(BF16)
    placed = nt(packed, place)
    colpart = 32.0 * placed[0:NS] + placed[32 : 32 + NS]
    samppart = pltpu.roll(placed[64 : 64 + NS], 32, 1)
    dests = jnp.zeros((1, W), I32)
    lane = iota((1, W), 1)
    dlane = 32 * lax.rem(mine + 2, 4)
    for j in range(NB):
        dests = jnp.where(lane == dlane + j, dest_s[j], dests)
    msg[:, 0, :] = colpart + samppart + dests.astype(F32)

    loads[0].wait()
    hi, lo = split2(tbl[...])
    hl[hotc:cols, 0:W] = hi
    hl[hotc:cols, W : 2 * W] = lo
    offs = jnp.zeros((HOTD, ROWS), I32)
    hrow = iota((HOTD, ROWS), 0)
    for k in range(HOTD):
        offs = jnp.where(hrow == k, off_s[k], offs)
    picked = nn(onehot(offs == iota((HOTD, ROWS), 1)), hl[hotc:cols, :])
    hotloc[...] = picked[:, :W] + picked[:, W:]
    for r in range(BLK):
        abuf[r] = tbl[pl.ds(r, NB, stride=BLK), :]

    def tell(sem):
        pl.semaphore_signal(sem, inc=1, device_id={"shard": sib}, device_id_type=MESH)

    @pl.when(core == 0)
    def _():
        pl.semaphore_wait(barrier, NS - 1)
        tell(column_sem)

    @pl.when(core == 1)
    def _():
        pl.semaphore_wait(column_sem, 1)

    pltpu.make_async_copy(msg.at[pl.ds(me, 1)], req.at[pl.ds(mine, 1)], req_recv).start()

    far_first(me, NS, lambda peer: pltpu.make_async_remote_copy(
        src_ref=msg.at[pl.ds(peer, 1)], dst_ref=req.at[pl.ds(mine, 1)],
        send_sem=req_send, recv_sem=req_recv,
        device_id={"shard": peer}, device_id_type=MESH,
    ).start())

    def push(src, dst, send_sem, recv_sem, peer):
        pltpu.make_async_remote_copy(
            src_ref=src, dst_ref=dst, send_sem=send_sem, recv_sem=recv_sem,
            device_id={"shard": peer}, device_id_type=MESH,
        ).start()

    def relay(peer, start, count):
        src = abuf.at[pl.ds(first_row(peer) + start, count)]
        dst = xbuf.at[
            start : start + count, pl.ds(pl.multiple_of(me * NB, NB), NB), :
        ]
        return src, dst

    def by_count(peer, act):
        @pl.when(lax.rem(peer, 3) < 2)
        def _():
            act(3)

        @pl.when(lax.rem(peer, 3) == 2)
        def _():
            act(2)

    pltpu.make_async_copy(*relay(me, 0, 1), one_recv.at[0]).start()
    pltpu.make_async_copy(*relay(me, 1, 1), one_recv.at[1]).start()

    @pl.when(three)
    def _():
        pltpu.make_async_copy(*relay(me, 2, 1), one_recv.at[2]).start()

    far_first(
        me, NS, lambda peer: push(*relay(peer, 0, 1), one_send, one_recv.at[0], peer)
    )
    far_first(
        me, NS, lambda peer: push(*relay(peer, 1, 1), one_send, one_recv.at[1], peer)
    )

    def third(peer):
        @pl.when(lax.rem(peer, 3) < 2)
        def _():
            push(*relay(peer, 2, 1), one_send, one_recv.at[2], peer)

    far_first(me, NS, third)

    @pl.when(core == 1)
    def _():
        pl.semaphore_wait(barrier, 2 * ng - 1)
        tell(plane_sem)

    @pl.when(core == 0)
    def _():
        pl.semaphore_wait(plane_sem, 1)

    hot_here = hotbuf.at[pl.ds(pl.multiple_of(grp * HOTD, HOTD), HOTD)]
    pltpu.make_async_copy(hotloc, hot_here, hot_recv).start()

    far_first_plane(grp, ng, lambda peer: pltpu.make_async_remote_copy(
        src_ref=hotloc, dst_ref=hot_here, send_sem=hot_send, recv_sem=hot_recv,
        device_id={"grp": peer}, device_id_type=MESH,
    ).start())

    wait_bytes(req, req_recv)
    asked = req[:, 0, :]
    b = iota((W, NBLK), 1)
    bs = (((b >> 3) & 1) * NZ) + (b >> 4)
    dlanes = onehot(iota((W, NBLK), 0) == 32 * ((bs + 2) & 3) + (b & 7))
    bs24 = bs[0:NS]
    target = jnp.sum(
        jnp.where(iota((NS, NBLK), 0) == bs24, nn(asked.astype(BF16), dlanes), 0.0),
        axis=0, keepdims=True,
    ).astype(I32)
    goes = jnp.where(iota((32, NBLK), 0) == target, 1.0, 0.0)
    earlier = onehot(iota((NBLK, NBLK), 0) < iota((NBLK, NBLK), 1))
    seat = nn(goes.astype(BF16), earlier) + (NB * iota((32, NBLK), 0)).astype(F32)
    seat = jnp.sum(goes * seat, axis=0, keepdims=True).astype(I32)
    perm = onehot(iota((NBLK, NBLK), 0) == seat)

    def reorder(i):
        x = xbuf[i]
        hi = x.astype(BF16)
        rest = x - hi.astype(F32)
        mid = rest.astype(BF16)
        low = (rest - mid.astype(F32)).astype(BF16)
        y = nn(perm, jnp.concatenate([hi, mid, low], axis=1))
        ybuf[i] = (y[:, :W] + y[:, W : 2 * W]) + y[:, 2 * W :]

    def deliver(peer, start, count):
        src = ybuf.at[
            start : start + count, pl.ds(pl.multiple_of(peer * NB, NB), NB), :
        ]
        return src, moved.at[pl.ds(first_row(me) + start, count)]

    def deliver_all(start, count):
        pltpu.make_async_copy(*deliver(me, start, count), two_recv).start()
        far_first(
            me, NS,
            lambda peer: push(*deliver(peer, start, count), two_send, two_recv, peer),
        )

    wait_bytes(xbuf.at[0:1], one_recv.at[0])
    reorder(0)
    deliver_all(0, 1)

    who = iota((NS, W), 0)
    spot = (iota((NS, W), 1) >> 5) & 3
    first = jnp.where(spot == (who & 3), asked, 0.0)
    second = pltpu.roll(jnp.where(spot == ((who + 1) & 3), asked, 0.0), W - 32, 1)
    pad = jnp.zeros((8 - GROUPS, W), F32)
    gather4 = lambda x: jnp.concatenate(
        [jnp.sum(x[4 * g : 4 * g + 4], axis=0, keepdims=True) for g in range(GROUPS)] + [pad],
        axis=0,
    )
    colv[...] = gather4(first).astype(I32)
    samp = gather4(second).astype(I32)
    keyv[...] = jnp.where(samp > 0, samp - 1 + ((iota((8, W), 1) >> 5) << 5), -1)

    @pl.loop(0, GROUPS)
    def _(g):
        key = keyv[pl.ds(g, 1), :]
        want = colv[pl.ds(g, 1), :]
        sums = onehot(iota((W, W), 0) == key)
        names = onehot(iota((cols, W), 0) == want)
        cmat[pl.ds(pl.multiple_of(g * W, W), W), :] = nt(sums, names).astype(BF16)


    wait_bytes(xbuf.at[1:2], one_recv.at[1])
    reorder(1)
    deliver_all(1, 1)

    wait_bytes(hotbuf, hot_recv)
    hi, lo = split2(hotbuf[...])
    hl[0:hotc, 0:W] = hi
    hl[0:hotc, W : 2 * W] = lo
    half = NZ * SAMP
    for h in range(2):
        part = nn(cmat[half * h : half * (h + 1), :], hl[...])
        pbuf[h] = (part[:, :W] + part[:, W:]).reshape(NZ, SAMP, W)
    to_sib = pltpu.make_async_remote_copy(
        src_ref=pbuf.at[1 - core], dst_ref=sbuf, send_sem=sib_send, recv_sem=sib_recv,
        device_id={"shard": sib}, device_id_type=MESH,
    )
    to_sib.start()
    to_sib.wait_recv()
    pbuf[core] += sbuf[...]
    pltpu.make_async_copy(pbuf.at[core, chip], pin.at[HOP], sum_recv).start()

    def chip_at(step):
        return lax.rem(chip + step + NZ, NZ)

    def send_sum(step, via, dst, recv_sem):
        push(
            pbuf.at[core, chip_at(step)], dst, sum_send, recv_sem,
            2 * chip_at(via) + core,
        )

    send_sum(6, 3 + 6 * core, rin.at[4], far_recv)
    for i, step in enumerate((-5, 5, -4, 4)):
        send_sum(step, step - HOP if step > 0 else step + HOP, rin.at[i], far_recv)


    @pl.when(three)
    def _():
        wait_bytes(xbuf.at[2:3], one_recv.at[2])
        reorder(2)
        deliver_all(2, 1)

    for step in (-2, 2, -1, 1):
        send_sum(step, step, pin.at[HOP + step], sum_recv)

    wait_bytes(rin, far_recv)
    pbuf[core, chip_at(-HOP)] += rin[0] + rin[2]
    pbuf[core, chip_at(HOP)] += rin[1] + rin[3]
    pbuf[core, chip_at(HOP + 6 * core)] += rin[4]
    for step in (-HOP, HOP):
        send_sum(step, step, pin.at[HOP + step], sum_recv)
    wait_bytes(pin, sum_recv)
    total = pin[0]
    for z in range(1, 2 * HOP + 1):
        total += pin[z]
    pooled[...] = total / lens.astype(F32)

    wait_bytes(moved, two_recv)
    to_sib.wait_send()
    wait_bytes(req.at[0 : NS - 1], req_send)
    wait_bytes(hotbuf.at[0 : hotc - HOTD], hot_send)
    wait_bytes(pbuf.at[0, 0 : NZ - 1], sum_send)

    by_count(me, lambda n: wait_bytes(abuf.at[0 : BLK - n], one_send))
    by_count(me, lambda n: wait_bytes(xbuf.at[0:n, 0 : NBLK - NB, :], two_send))


def finish(moved, sums, table, pooled, rows, sem):
    small = pltpu.make_async_copy(sums, pooled, sem.at[1])
    small.start()
    for k in range(NB):
        block = pl.ds(k * BLK, BLK)
        rows[block, :] = moved[:, k, :]
        pltpu.make_async_copy(rows.at[block], table.at[block], sem.at[0]).start()
    wait_bytes(rows, sem.at[0])
    small.wait()


def local(table, hot_offsets, cold_dest, bag_ids, bag_len):
    ng = lax.axis_size("grp")
    hotc = ng * HOTD
    cols = hotc + ROWS
    dma = pltpu.SemaphoreType.DMA
    moved, pooled = pl.pallas_call(
        functools.partial(kernel, ng),
        out_shape=(
            jax.ShapeDtypeStruct((BLK, NB, W), F32),
            jax.ShapeDtypeStruct((SAMP, W), F32),
        ),
        in_specs=[pl.BlockSpec(memory_space=pltpu.HBM)] * 5,
        out_specs=(
            pl.BlockSpec(memory_space=pl.ANY),
            pl.BlockSpec(memory_space=pltpu.VMEM),
        ),
        scratch_shapes=[
            pltpu.VMEM((ROWS, W), F32),
            pltpu.VMEM((BAG, SAMP), I32),
            pltpu.SMEM((HOTD,), I32),
            pltpu.SMEM((NB,), I32),
            pltpu.SMEM((SAMP,), I32),
            pltpu.VMEM((BLK, NB, W), F32),
            pltpu.VMEM((cols, 2 * W), BF16),
            pltpu.VMEM((HOTD, W), F32),
            pltpu.VMEM((hotc, W), F32),
            pltpu.VMEM((NS, 1, W), F32),
            pltpu.VMEM((NS, 1, W), F32),
            pltpu.VMEM((3, NBLK, W), F32),
            pltpu.VMEM((3, NBLK, W), F32),
            pltpu.VMEM((NS * SAMP, cols), BF16),
            pltpu.VMEM((2, NZ, SAMP, W), F32),
            pltpu.VMEM((NZ, SAMP, W), F32),
            pltpu.VMEM((5, SAMP, W), F32),
            pltpu.VMEM((2 * HOP + 1, SAMP, W), F32),
            pltpu.VMEM((8, W), I32),
            pltpu.VMEM((8, W), I32),
            dma((5,)),
        ]
        + [dma(())] * 5
        + [dma((3,))]
        + [dma(())] * 7
        + [pltpu.SemaphoreType.REGULAR] * 2,
        compiler_params=pltpu.CompilerParams(
            collective_id=0, has_side_effects=True, vmem_limit_bytes=24 * 1024 * 1024
        ),
    )(
        *(
            pltpu.with_memory_space_constraint(x, pltpu.HBM)
            for x in (table, hot_offsets, cold_dest, bag_ids.T, bag_len)
        )
    )
    return pl.pallas_call(
        finish,
        out_shape=(
            jax.ShapeDtypeStruct((ROWS, W), F32),
            jax.ShapeDtypeStruct((SAMP, W), F32),
        ),
        in_specs=[pl.BlockSpec(memory_space=pltpu.VMEM)] * 2,
        out_specs=[pl.BlockSpec(memory_space=pltpu.HBM)] * 2,
        scratch_shapes=[pltpu.VMEM((ROWS, W), F32), pltpu.SemaphoreType.DMA((2,))],
    )(
        pltpu.with_memory_space_constraint(moved, pltpu.VMEM),
        pltpu.with_memory_space_constraint(pooled, pltpu.VMEM),
    )


def solution(mesh):
    return jax.shard_map(
        local,
        mesh=mesh,
        in_specs=(
            P(("grp", "shard"), None),
            P(("grp", "shard")),
            P(("grp", "shard")),
            P(("grp", "shard"), None),
            P(("grp", "shard")),
        ),
        out_specs=(P(("grp", "shard"), None), P(("grp", "shard"), None)),
        check_vma=False,
    )
```
